32 devices in a mesh: wide: 8 (over z, y), narrow: 4 (over x, core).
Axes of the slice: x: 2, y: 2, z: 4, core: 2. Of those that a mesh axis runs over, the one named last changes fastest.
Arguments:
- section_input: bfloat16 [16384, 256], P(('wide', 'narrow')), may hold values from -40 to 40
- mid_features: bfloat16 [16384, 256], P(('wide', 'narrow')), may hold values from -40 to 40
- out_grad: bfloat16 [16384, 256], P(('wide', 'narrow')), may hold values from -6 to 6
- to_hilbert: int32 [16384], P(('wide', 'narrow')), may hold values from 0 to 16383, as said below
- to_zorder: int32 [16384], P(('wide', 'narrow')), may hold values from 0 to 16383, as said below
- qkv_weight: bfloat16 [2, 256, 768], replicated, may hold values from -0.6 to 0.6
- out_weight: bfloat16 [2, 256, 256], replicated, may hold values from -0.75 to 0.75
Outputs:
- input_grad: bfloat16 [16384, 256], P(('wide', 'narrow'))
- qkv_weight_grad: float32 [2, 256, 768], replicated
- out_weight_grad: float32 [2, 256, 256], replicated
The draws below stay inside these ranges and needn't reach their ends.
Inputs may be any that keep to these rules, and one draw needn't show every extreme that they name: to_hilbert is a permutation of the 16384 points. The devices form 8 aligned groups of 4 consecutive devices (octants of the scan); the points of one group in z-order are exactly the points of one group in Hilbert order, the pairing of groups drawn from the seed. Between a z-order device and a Hilbert-order device of paired groups at least 64 and at most 192 points move, the most reached in every draw; between unpaired groups none. to_zorder is the inverse permutation of to_hilbert.
All inputs are finite; a program needn't handle non-finite values.
Results may differ from the reference program's by a relative error of at most 0.011.
The reference program's roundings to bfloat16 on the way count: a program that leaves them out, or rounds other values in their place, can miss the bound.
Values may be sent and summed in bfloat16 or wider, within the bound.
No kernel may reach another device: no remote copies, remote signals or barrier semaphores. Data moves between devices by JAX's collectives and lax.ppermute only.
A program may use at most 64 MiB of HBM per device.

```python
import math
from functools import partial
import jax
import jax.numpy as jnp
from jax import lax

C = 256
HEADS = 16
PATCH = 512
LAYERS = 2
P_DEV = 512
POINTS = 16384
GROUP = 4
BASE = 128
SPREAD = 32
DEVICES = 32


def build_orders(key):
    base_key = jax.random.fold_in(key, 17)
    key_load, key_recv, key_send, key_pair = jax.random.split(base_key, 4)
    offsets_grid = jax.random.randint(key_load, (8, GROUP, GROUP), 0, SPREAD + 1)
    offsets_grid = offsets_grid.at[:, 0, 0].set(SPREAD).at[:, 1, 1].set(SPREAD)
    offsets_grid = offsets_grid.at[:, 1, 0].set(0).at[:, 0, 1].set(0)
    shifted = jnp.roll(offsets_grid, -1, 1)
    local_counts = BASE + offsets_grid - shifted - jnp.roll(offsets_grid, -1, 2) + jnp.roll(shifted, -1, 2)
    free_octants = jnp.array([2, 3, 5, 6, 7], jnp.int32)
    mixed_octants = jax.random.permutation(key_pair, free_octants)
    pairing = jnp.zeros((8,), jnp.int32).at[free_octants].set(mixed_octants)
    pairing = pairing.at[0].set(4).at[4].set(0).at[1].set(1)
    device_ids = jnp.arange(DEVICES, dtype=jnp.int32)
    source_group = device_ids[:, None] // GROUP
    target_group = device_ids[None, :] // GROUP
    source_local = device_ids[:, None] % GROUP
    target_local = device_ids[None, :] % GROUP
    paired = (target_group == pairing[source_group]).astype(jnp.int32)
    counts = paired * local_counts[source_group, source_local, target_local]
    col_start = jnp.cumsum(counts, axis=0) - counts
    row_start = jnp.cumsum(counts, axis=1) - counts
    recv_perm = jax.vmap(lambda sub_key: jax.random.permutation(sub_key, P_DEV))(jax.random.split(key_recv, DEVICES))
    send_perm = jax.vmap(lambda sub_key: jax.random.permutation(sub_key, P_DEV))(jax.random.split(key_send, DEVICES))

    def one_device(target):
        slot_ids = recv_perm[target]
        starts = col_start[:, target]
        ends = starts + counts[:, target]
        inside = (starts[None, :] <= slot_ids[:, None]) & (slot_ids[:, None] < ends[None, :])
        source = jnp.sum(inside.astype(jnp.int32) * device_ids[None, :], axis=1)
        within = slot_ids - starts[source]
        send_slot = row_start[source, target] + within
        return source * P_DEV + send_perm[source, send_slot]
    to_hilbert = lax.map(one_device, device_ids).reshape(-1).astype(jnp.int32)
    to_zorder = jnp.zeros((POINTS,), jnp.int32).at[to_hilbert].set(jnp.arange(POINTS, dtype=jnp.int32))
    return (to_hilbert, to_zorder)


def draw_to_hilbert(key, part):
    return build_orders(key)[0]


def draw_to_zorder(key, part):
    return build_orders(key)[1]


def draw_rows(key):
    key_scale, key_base = jax.random.split(key, 2)
    row_scale = jnp.exp(jax.random.uniform(key_scale, (POINTS, 1), jnp.float32, math.log(0.5), math.log(2.0)))
    base_rows = jax.random.normal(key_base, (POINTS, C), jnp.float32) * row_scale
    return jnp.clip(base_rows, -40.0, 40.0).astype(jnp.bfloat16)


def draw_section_input(key, part):
    return draw_rows(jax.random.fold_in(key, 1))


def draw_mid_features(key, part):
    return draw_rows(jax.random.fold_in(key, 2))


def draw_qkv_weight(key, part):
    key_main = jax.random.fold_in(jax.random.fold_in(key, 3), 0)
    weights = jax.random.normal(key_main, (LAYERS, C, 3 * C), jnp.float32) * (1.5 / math.sqrt(C))
    return jnp.clip(weights, -0.59375, 0.59375).astype(jnp.bfloat16)


def block_scale(stream_key, shape, pieces, least, high):
    gain = 1.0
    for axis_at, parts in pieces:
        steps = jax.random.uniform(jax.random.fold_in(jax.random.fold_in(stream_key, 6), axis_at), (parts,), jnp.float32, least / len(pieces), high / len(pieces))
        gain = gain * jnp.repeat(jnp.exp(steps), shape[axis_at] // parts).reshape((-1,) + (1,) * (len(shape) - 1 - axis_at))
    return gain


def bell_draw(own_key, extent, spread, reach, cuts=(), kind=jnp.bfloat16):
    result = jax.random.normal(own_key, extent, jnp.float32) * spread
    if len(cuts) > 0:
        result = block_scale(own_key, extent, cuts, -0.22, 0.18) * result
    return jnp.clip(result, min=-reach, max=reach).astype(kind)


def setup_inputs(seed: int = 0) -> dict:
    seeds = jax.random.split(jax.random.key(seed), 8)
    return {
        "section_input": draw_section_input(jax.random.fold_in(seeds[7], 71), 0),
        "mid_features": draw_mid_features(jax.random.fold_in(seeds[7], 71), 0),
        "out_grad": bell_draw(seeds[2], (POINTS, C), 1.0, 6.0, ((0, 32),)),
        "to_hilbert": draw_to_hilbert(jax.random.fold_in(seeds[7], 71), 0),
        "to_zorder": draw_to_zorder(jax.random.fold_in(seeds[7], 71), 0),
        "qkv_weight": draw_qkv_weight(jax.random.fold_in(seeds[7], 71), 0),
        "out_weight": bell_draw(seeds[6], (LAYERS, C, C), (C // 4) ** -0.5, 0.75),
    }


def head_backward(inputs, score_scale):
    queries, key_rows, values, delta_out = inputs
    scores = jnp.dot(queries, key_rows.T, preferred_element_type=jnp.float32) * score_scale
    row_peak = jnp.max(scores, axis=-1, keepdims=True)
    powers = jnp.exp(scores - row_peak)
    weights = powers / jnp.sum(powers, axis=-1, keepdims=True)
    weights_half = weights.astype(jnp.bfloat16)
    attended = jnp.dot(weights_half, values, preferred_element_type=jnp.float32).astype(jnp.bfloat16)
    weight_grad = jnp.dot(delta_out, values.T, preferred_element_type=jnp.float32)
    centre = jnp.sum(weights * weight_grad, axis=-1, keepdims=True)
    score_grad = (weights * (weight_grad - centre) * score_scale).astype(jnp.bfloat16)
    query_grad = jnp.dot(score_grad, key_rows, preferred_element_type=jnp.float32)
    key_grad = jnp.dot(score_grad.T, queries, preferred_element_type=jnp.float32)
    value_grad = jnp.dot(weights_half.T, delta_out, preferred_element_type=jnp.float32)
    return attended, jnp.stack([query_grad, key_grad, value_grad]).astype(jnp.bfloat16)


def patch_backward(features, gradients, qkv_w, out_w):
    rows_count, channels = features.shape
    head_size = channels // HEADS
    score_scale = head_size ** -0.5
    projected = jnp.dot(features, qkv_w, preferred_element_type=jnp.float32).astype(jnp.bfloat16)
    split_heads = projected.reshape(rows_count, 3, HEADS, head_size).transpose(1, 2, 0, 3)
    out_delta = jnp.dot(gradients, out_w.T, preferred_element_type=jnp.float32).astype(jnp.bfloat16)
    out_delta = out_delta.reshape(rows_count, HEADS, head_size).transpose(1, 0, 2)
    attended, qkv_delta = lax.map(partial(head_backward, score_scale=score_scale),
                                  (split_heads[0], split_heads[1], split_heads[2], out_delta))
    mixed_heads = attended.transpose(1, 0, 2).reshape(rows_count, channels)
    qkv_flat = qkv_delta.transpose(2, 1, 0, 3).reshape(rows_count, 3 * channels)
    out_w_grad = jnp.dot(mixed_heads.T, gradients, preferred_element_type=jnp.float32)
    qkv_w_grad = jnp.dot(features.T, qkv_flat, preferred_element_type=jnp.float32)
    feature_grad = jnp.dot(qkv_flat, qkv_w.T, preferred_element_type=jnp.float32)
    return feature_grad, qkv_w_grad, out_w_grad


def layer_backward(features, gradients, qkv_w, out_w):
    rows_total, channels = features.shape
    feat_blocks = features.reshape(-1, PATCH, channels)
    grad_blocks = gradients.reshape(-1, PATCH, channels)

    def step_fn(running, inputs_pair):
        feature_grad, qkv_w_grad, out_w_grad = patch_backward(inputs_pair[0], inputs_pair[1], qkv_w, out_w)
        return (running[0] + qkv_w_grad, running[1] + out_w_grad), feature_grad

    zero_sums = (jnp.zeros((channels, 3 * channels), jnp.float32), jnp.zeros((channels, channels), jnp.float32))
    totals, feature_grads = lax.scan(step_fn, zero_sums, (feat_blocks, grad_blocks))
    return feature_grads.reshape(rows_total, channels), totals[0], totals[1]


def reference(section_input, mid_features, out_grad, to_hilbert, to_zorder, qkv_weight, out_weight):
    grad_scale = POINTS ** -0.5
    late_grad, late_qkv, late_out = layer_backward(mid_features, out_grad, qkv_weight[1], out_weight[1])
    mid_grad = (out_grad.astype(jnp.float32) + late_grad).astype(jnp.bfloat16)
    early_grad, early_qkv, early_out = layer_backward(section_input[to_hilbert], mid_grad[to_hilbert],
                                                      qkv_weight[0], out_weight[0])
    early_half = lax.optimization_barrier(early_grad.astype(jnp.bfloat16))
    input_grad = (mid_grad.astype(jnp.float32) + early_half[to_zorder].astype(jnp.float32)).astype(jnp.bfloat16)
    qkv_weight_grad = jnp.stack([early_qkv, late_qkv]) * grad_scale
    out_weight_grad = jnp.stack([early_out, late_out]) * grad_scale
    return input_grad, qkv_weight_grad, out_weight_grad
```

```python
from functools import partial

import jax
import jax.numpy as jnp
from jax import lax
from jax.experimental import pallas as pl
from jax.experimental.pallas import tpu as pltpu
from jax.sharding import PartitionSpec as P

HEADS = 16
LOG2E = 1.4426950408889634
f32, bf16 = jnp.float32, jnp.bfloat16
AXES = ("wide", "narrow")
VMEM_LIMIT = 48 * 2**20


def dg(a, b, contract_a, contract_b):
    return lax.dot_general(
        a, b, (((contract_a,), (contract_b,)), ((), ())), preferred_element_type=f32
    )


def whole(*_):
    return pl.BlockSpec(memory_space=pltpu.VMEM)


def scalar_spec():
    return pl.BlockSpec(memory_space=pltpu.SMEM)


def call(body, out_shape, n_in, scratch=(), flops=0):
    n_out = len(out_shape)
    return pl.pallas_call(
        body,
        out_shape=tuple(out_shape),
        in_specs=[scalar_spec()] + [whole()] * (n_in - 1),
        out_specs=tuple([whole()] * n_out),
        scratch_shapes=list(scratch),
        compiler_params=pltpu.CompilerParams(vmem_limit_bytes=VMEM_LIMIT),
        cost_estimate=pl.CostEstimate(flops=flops, bytes_accessed=2**20, transcendentals=0),
    )


def slot_matrix(slots, first, count):
    rows = slots.shape[1]
    at = lax.broadcasted_iota(jnp.int32, (count, rows), 0) + first
    return (at == slots).astype(f32).astype(bf16)


def route_kernel(group, cap, me_ref, tz_ref, rows_ref, slots_ref, *send_refs):
    n, channels = rows_ref.shape
    here = me_ref[0] % group
    target = tz_ref[...]
    partner = (target // n % group) ^ here
    spot = target % n
    lanes = max(16, group)
    which = lax.broadcasted_iota(jnp.int32, (lanes, n), 0)
    mine = (which == partner).astype(f32)
    earlier = (
        lax.broadcasted_iota(jnp.int32, (n, n), 0) < lax.broadcasted_iota(jnp.int32, (n, n), 1)
    ).astype(f32).astype(bf16)
    before = dg(mine.astype(bf16), earlier, 1, 0)
    rank = jnp.sum(mine * before, axis=0, keepdims=True).astype(jnp.int32)
    slots = partner * cap + rank
    slots_ref[...] = slots
    row_at = lax.broadcasted_iota(jnp.int32, (16, n), 0)
    info = jnp.where(
        row_at == 0, spot % 256, jnp.where(row_at == 1, spot // 256, (row_at == 2).astype(jnp.int32))
    ).astype(f32).astype(bf16)
    rows = rows_ref[...]
    for s in range(group):
        chosen = slot_matrix(slots, s * cap, cap)
        send_refs[s][0:cap, :] = dg(chosen, rows, 1, 0).astype(bf16)
        where = dg(info, chosen, 1, 1)
        if cap < channels:
            where = jnp.concatenate([where, jnp.zeros((16, channels - cap), f32)], axis=1)
        send_refs[s][cap : cap + 16, :] = where.astype(bf16)


def spots_of(recv_ref, cap):
    info = recv_ref[cap : cap + 16, 0:cap].astype(f32)
    spot = info[0:1] + 256.0 * info[1:2] + 1024.0 * (info[2:3] - 1.0)
    return spot.astype(jnp.int32)


def place_matrix(spot, n):
    at = lax.broadcasted_iota(jnp.int32, (n, spot.shape[1]), 0)
    return (at == spot).astype(f32).astype(bf16)


def one_head(proj, delta, head, n, channels, size):
    at = pl.multiple_of(head * size, size)
    q = proj[pl.ds(at, size), :]
    k = proj[pl.ds(channels + at, size), :]
    v = proj[pl.ds(2 * channels + at, size), :]
    o = proj[pl.ds(3 * channels + at, size), :]
    score_scale = size**-0.5
    scores = dg(k, q, 0, 0)
    peak = jnp.max(scores, axis=0, keepdims=True)
    powers = jnp.exp2((scores - peak) * (score_scale * LOG2E))
    weights = powers * (1.0 / jnp.sum(powers, axis=0, keepdims=True))
    half = weights.astype(bf16)
    weight_grad = dg(v, o, 0, 0)
    centre = jnp.sum(weights * weight_grad, axis=0, keepdims=True)
    score_grad = (weights * (weight_grad - centre)).astype(bf16)
    delta[pl.ds(at, size), :] = (dg(k, score_grad, 1, 0) * score_scale).astype(bf16)
    delta[pl.ds(channels + at, size), :] = (dg(q, score_grad, 1, 1) * score_scale).astype(bf16)
    delta[pl.ds(2 * channels + at, size), :] = dg(o, half, 1, 1).astype(bf16)
    delta[pl.ds(3 * channels + at, size), :] = dg(v, half, 1, 0).astype(bf16)


def layer(me, h, g, qkv_w, out_w, proj, delta, sums_ref):
    n, channels = h.shape
    size = channels // HEADS
    proj[0 : 3 * channels, :] = dg(qkv_w, h, 0, 1).astype(bf16)
    proj[3 * channels : 4 * channels, :] = dg(out_w, g, 1, 1).astype(bf16)

    def step(head, carry):
        one_head(proj, delta, head, n, channels, size)
        return carry

    lax.fori_loop(0, HEADS, step, 0)
    qkv_delta = delta[0 : 3 * channels, :]
    qkv_grad = dg(h.T, qkv_delta, 1, 1)
    out_grad = dg(delta[3 * channels : 4 * channels, :], g, 1, 0)
    chunks, rows, _ = sums_ref.shape
    per = channels // rows
    for c in range(chunks):
        part, start = c // per, (c % per) * rows
        if part < 3:
            piece = qkv_grad[start : start + rows, part * channels : (part + 1) * channels]
        else:
            piece = out_grad[start : start + rows, :]
        sums_ref[c ^ me] = piece.astype(bf16)
    return dg(qkv_w, qkv_delta, 1, 0).T


def late_kernel(group, cap, me_ref, h_ref, g_ref, qkv_ref, out_ref, slots_ref, *rest):
    mid_ref, sums_ref = rest[0], rest[1]
    send_refs = rest[2 : 2 + group]
    proj, delta = rest[2 + group :]
    g = g_ref[...]
    row_grad = layer(me_ref[0], h_ref[...], g, qkv_ref[1], out_ref[1], proj, delta, sums_ref)
    mid = (g.astype(f32) + row_grad).astype(bf16)
    mid_ref[...] = mid
    slots = slots_ref[...]
    for s in range(group):
        send_refs[s][...] = dg(slot_matrix(slots, s * cap, cap), mid, 1, 0).astype(bf16)


def early_kernel(group, cap, me_ref, qkv_ref, out_ref, *rest):
    feats_refs = rest[0:group]
    grads_refs = rest[group : 2 * group]
    sums_ref = rest[2 * group]
    send_refs = rest[2 * group + 1 : 3 * group + 1]
    proj, delta = rest[3 * group + 1 :]
    n, channels = proj.shape[1], feats_refs[0].shape[1]
    h = jnp.zeros((n, channels), f32)
    g = jnp.zeros((n, channels), f32)
    spots = []
    for s in range(group):
        spot = spots_of(feats_refs[s], cap)
        spots.append(spot)
        place = place_matrix(spot, n)
        h = h + dg(place, feats_refs[s][0:cap, :], 1, 0)
        g = g + dg(place, grads_refs[s][...], 1, 0)
    h, g = h.astype(bf16), g.astype(bf16)
    row_grad = layer(me_ref[0], h, g, qkv_ref[0], out_ref[0], proj, delta, sums_ref)
    early = row_grad.astype(bf16)
    for s in range(group):
        send_refs[s][...] = dg(place_matrix(spots[s], n), early, 0, 0).astype(bf16)


def join_kernel(group, cap, me_ref, slots_ref, mid_ref, *rest):
    back_refs, input_ref = rest[:group], rest[group]
    slots = slots_ref[...]
    total = jnp.zeros(mid_ref.shape, f32)
    for s in range(group):
        total = total + dg(slot_matrix(slots, s * cap, cap), back_refs[s][...], 0, 0)
    input_ref[...] = (mid_ref[...].astype(f32) + total.astype(bf16).astype(f32)).astype(bf16)


def finish_kernel(scale, me_ref, early_ref, late_ref, qkv_ref, out_ref):
    me = me_ref[0]
    chunks, rows, channels = early_ref.shape
    per = channels // rows
    for l, ref in enumerate((early_ref, late_ref)):
        for c in range(chunks):
            part, start = c // per, (c % per) * rows
            piece = ref[c ^ me].astype(f32) * scale
            if part < 3:
                qkv_ref[l, start : start + rows, part * channels : (part + 1) * channels] = piece
            else:
                out_ref[l, start : start + rows, :] = piece


def swap(x, mask, devices):
    return lax.ppermute(x, AXES, [(d, d ^ mask) for d in range(devices)])


def exchange(blocks, devices):
    return [blocks[0]] + [swap(blocks[s], s, devices) for s in range(1, len(blocks))]


def stage_masks(bits):
    masks = [0]
    for b in bits:
        masks = masks + [m | (1 << b) for m in masks]
    return masks


def sum_everywhere(x, stages, devices):
    tail = x.shape[1:]
    live = list(range(len(stages)))
    for bits in stages:
        masks = stage_masks(bits)
        parts = x.reshape((len(masks), -1) + tail)
        got = [parts[0]] + [swap(parts[i], masks[i], devices) for i in range(1, len(masks))]
        x = sum(p.astype(f32) for p in got).astype(bf16)
    for bits in reversed(stages):
        masks = stage_masks(bits)
        got = [x] + [swap(x, m, devices) for m in masks[1:]]
        x = jnp.concatenate(got, axis=0)
    return x


def plan_stages(mesh_shape, core_first):
    return core_first


def on_device(stages, section_input, mid_features, out_grad, to_hilbert, to_zorder, qkv_weight, out_weight):
    devices = lax.axis_size("wide") * lax.axis_size("narrow")
    n, channels = section_input.shape
    group = devices // 8
    share = n // group
    cap = share + 2 * (share // 4)
    rank = lax.axis_index("wide") * lax.axis_size("narrow") + lax.axis_index("narrow")
    me = rank.astype(jnp.int32).reshape(1)
    order = [b for bits in stages for b in reversed(bits)]
    total_bits = len(order)
    place = jnp.int32(0)
    for i, b in enumerate(order):
        place = place | (((rank >> b) & 1) << (total_bits - 1 - i))
    place = place.astype(jnp.int32).reshape(1)

    rows_s = jax.ShapeDtypeStruct((n, channels), bf16)
    send_s = jax.ShapeDtypeStruct((cap, channels), bf16)
    chunk_rows = 4 * channels // devices
    sums_s = jax.ShapeDtypeStruct((devices, chunk_rows, channels), bf16)
    scratch = [pltpu.VMEM((4 * channels, n), bf16), pltpu.VMEM((4 * channels, n), bf16)]

    slots, *feats = call(
        partial(route_kernel, group, cap),
        [jax.ShapeDtypeStruct((1, n), jnp.int32)]
        + [jax.ShapeDtypeStruct((cap + 16, channels), bf16)] * group,
        3,
        flops=10**9,
    )(me, to_zorder.reshape(1, n), section_input)
    feats = exchange(feats, devices)
    mid, late_sums, *grads = call(
        partial(late_kernel, group, cap),
        [rows_s, sums_s] + [send_s] * group,
        6,
        scratch,
        flops=2 * 10**10,
    )(place, mid_features, out_grad, qkv_weight, out_weight, slots)
    grads = exchange(grads, devices)
    early_sums, *backs = call(
        partial(early_kernel, group, cap),
        [sums_s] + [send_s] * group,
        3 + 2 * group,
        scratch,
        flops=2 * 10**10,
    )(place, qkv_weight, out_weight, *feats, *grads)
    backs = exchange(backs, devices)
    late_total = sum_everywhere(late_sums, stages, devices)
    early_total = sum_everywhere(early_sums, stages, devices)
    (input_grad,) = call(partial(join_kernel, group, cap), [rows_s], 3 + group, flops=10**9)(
        me, slots, mid, *backs
    )
    qkv_grad, out_w_grad = call(
        partial(finish_kernel, float((n * devices) ** -0.5)),
        [jax.ShapeDtypeStruct(qkv_weight.shape, f32), jax.ShapeDtypeStruct(out_weight.shape, f32)],
        3,
        flops=10**8,
    )(place, early_total, late_total)
    return (input_grad, qkv_grad, out_w_grad)


def solution(mesh):
    devices = mesh.size
    bits = devices.bit_length() - 1
    stages = [(0,)] + [tuple(range(b, min(b + 2, bits))) for b in range(1, bits, 2)]
    placed = (
        P(AXES, None),
        P(AXES, None),
        P(AXES, None),
        P(AXES),
        P(AXES),
        P(),
        P(),
    )
    return jax.shard_map(
        partial(on_device, stages),
        mesh=mesh,
        in_specs=placed,
        out_specs=(P(AXES, None), P(), P()),
        check_vma=False,
    )
```

```python
from functools import partial

import jax
import jax.numpy as jnp
from jax import lax
from jax.experimental import pallas as pl
from jax.experimental.pallas import tpu as pltpu
from jax.sharding import PartitionSpec as P

HEADS = 16
LOG2E = 1.4426950408889634
f32, bf16, i32 = jnp.float32, jnp.bfloat16, jnp.int32
AXES = ("wide", "narrow")
VMEM_LIMIT = 28 * 2**20


def shape(dims, dtype):
    return jax.ShapeDtypeStruct(tuple(dims), dtype)


def dg(a, b, contract_a, contract_b):
    return lax.dot_general(
        a, b, (((contract_a,), (contract_b,)), ((), ())), preferred_element_type=f32
    )


def call(body, out_shape, args, scratch=(), us=1):
    return pl.pallas_call(
        body,
        out_shape=tuple(out_shape),
        in_specs=[pl.BlockSpec(memory_space=pltpu.SMEM)]
        + [pl.BlockSpec(memory_space=pltpu.VMEM)] * (len(args) - 1),
        out_specs=tuple([pl.BlockSpec(memory_space=pltpu.VMEM)] * len(out_shape)),
        scratch_shapes=list(scratch),
        compiler_params=pltpu.CompilerParams(vmem_limit_bytes=VMEM_LIMIT),
        cost_estimate=pl.CostEstimate(flops=us * 10**9, bytes_accessed=2**20, transcendentals=0),
    )(*args)


def slot_matrix(slots, first, count):
    rows = slots.shape[1]
    at = lax.broadcasted_iota(i32, (count, rows), 0) + first
    return (at == slots).astype(f32).astype(bf16)


def place_matrix(spot, n):
    at = lax.broadcasted_iota(i32, (n, spot.shape[1]), 0)
    return (at == spot).astype(f32).astype(bf16)


def spots_of(recv_ref, cap):
    info = recv_ref[cap : cap + 16, 0:cap].astype(f32)
    spot = info[0:1] + 256.0 * info[1:2] + 1024.0 * (info[2:3] - 1.0)
    return spot.astype(i32)


def route_kernel(group, cap, me_ref, tz_ref, rows_ref, slots_ref, *send_refs):
    n, channels = rows_ref.shape
    here = me_ref[0] % group
    target = tz_ref[...]
    partner = (target // n % group) ^ here
    spot = target % n
    lanes = max(16, group)
    which = lax.broadcasted_iota(i32, (lanes, n), 0)
    mine = (which == partner).astype(f32)
    earlier = (
        lax.broadcasted_iota(i32, (n, n), 0) < lax.broadcasted_iota(i32, (n, n), 1)
    ).astype(f32).astype(bf16)
    before = dg(mine.astype(bf16), earlier, 1, 0)
    rank = jnp.sum(mine * before, axis=0, keepdims=True).astype(i32)
    slots = partner * cap + rank
    slots_ref[...] = slots
    row_at = lax.broadcasted_iota(i32, (16, n), 0)
    info = jnp.where(
        row_at == 0, spot % 256, jnp.where(row_at == 1, spot // 256, (row_at == 2).astype(i32))
    ).astype(f32).astype(bf16)
    rows = rows_ref[...]
    for s in range(group):
        chosen = slot_matrix(slots, s * cap, cap)
        send_refs[s][0:cap, :] = dg(chosen, rows, 1, 0).astype(bf16)
        where = dg(info, chosen, 1, 1)
        if cap < channels:
            where = jnp.concatenate([where, jnp.zeros((16, channels - cap), f32)], axis=1)
        send_refs[s][cap : cap + 16, :] = where.astype(bf16)


def two_terms(x):
    high = x.astype(bf16)
    return jnp.concatenate([high, (x - high.astype(f32)).astype(bf16)], axis=0)


def forward_heads(heads, channels, size, proj, powers_ref, att_ref, inv_ref):
    every = range(len(heads))
    at = [pl.multiple_of(h * size, size) for h in heads]
    q = [proj[pl.ds(r, size), :] for r in at]
    k = [proj[pl.ds(channels + r, size), :] for r in at]
    v = [proj[pl.ds(2 * channels + r, size), :] for r in at]
    k = [jnp.concatenate([x, x], axis=0) for x in k]
    q = [two_terms(x.astype(f32) * (size**-0.5 * LOG2E)) for x in q]
    scores = [dg(k[i], q[i], 0, 0) for i in every]
    peaks = [jnp.max(x, axis=0, keepdims=True) for x in scores]
    powers = [jnp.exp2(scores[i] - peaks[i]) for i in every]
    half = [x.astype(bf16) for x in powers]
    inverse = [1.0 / jnp.sum(x, axis=0, keepdims=True) for x in powers]
    attended = [dg(v[i], half[i], 1, 0) * inverse[i] for i in every]
    for i in every:
        powers_ref[heads[i]] = half[i]
        inv_ref[pl.ds(heads[i], 1), :] = inverse[i]
        att_ref[pl.ds(at[i], size), :] = attended[i]


def backward_heads(heads, channels, size, proj, out_delta, powers_ref, att_ref, inv_ref, delta):
    every = range(len(heads))
    at = [pl.multiple_of(h * size, size) for h in heads]
    q = [proj[pl.ds(r, size), :] for r in at]
    k = [proj[pl.ds(channels + r, size), :] for r in at]
    v = [proj[pl.ds(2 * channels + r, size), :] for r in at]
    o = [out_delta[pl.ds(r, size), :].astype(f32) for r in at]
    inverse = [inv_ref[pl.ds(h, 1), :] for h in heads]
    half = [powers_ref[h] for h in heads]
    centre = [
        jnp.sum(att_ref[pl.ds(at[i], size), :] * o[i], axis=0, keepdims=True) * inverse[i]
        for i in every
    ]
    o = [two_terms(o[i] * inverse[i]) for i in every]
    v = [jnp.concatenate([x, x], axis=0) for x in v]
    score_grad = [
        (half[i].astype(f32) * (dg(v[i], o[i], 0, 0) - centre[i])).astype(bf16) for i in every
    ]
    value = [dg(o[i], half[i], 1, 1) for i in every]
    query = [dg(k[i], score_grad[i], 1, 0) for i in every]
    key = [dg(q[i], score_grad[i], 1, 1) for i in every]
    scale = size**-0.5
    for i in every:
        delta[pl.ds(at[i], size), :] = (query[i] * scale).astype(bf16)
        delta[pl.ds(channels + at[i], size), :] = (key[i] * scale).astype(bf16)
        delta[pl.ds(2 * channels + at[i], size), :] = (value[i][0:size] + value[i][size:]).astype(bf16)


def loop_heads(steps, per, body):
    def step(i, carry):
        body([i * per + u for u in range(per)])
        return carry

    lax.fori_loop(0, steps // per, step, 0)


def late_kernel(group, cap, me_ref, h_ref, g_ref, qkv_ref, out_ref, slots_ref, *rest):
    mid_ref, sums_ref = rest[0], rest[1]
    send_refs = rest[2 : 2 + group]
    proj, delta, powers_ref, att_ref, inv_ref = rest[2 + group :]
    h, g = h_ref[...], g_ref[...]
    n, channels = h.shape
    size = channels // HEADS
    qkv_w = qkv_ref[1]
    proj[0 : 3 * channels, :] = dg(qkv_w, h, 0, 1).astype(bf16)
    proj[3 * channels : 4 * channels, :] = dg(out_ref[1], g, 1, 1).astype(bf16)
    out_delta = proj.at[3 * channels : 4 * channels, :]

    def body(heads):
        forward_heads(heads, channels, size, proj, powers_ref, att_ref, inv_ref)
        backward_heads(heads, channels, size, proj, out_delta, powers_ref, att_ref, inv_ref, delta)

    loop_heads(HEADS, 2, body)
    qkv_delta = delta[...]
    row_grad = dg(qkv_w, qkv_delta, 1, 0).T
    mid = (g.astype(f32) + row_grad).astype(bf16)
    mid_ref[...] = mid
    slots = slots_ref[...]
    for s in range(group):
        send_refs[s][...] = dg(slot_matrix(slots, s * cap, cap), mid, 1, 0).astype(bf16)
    att = att_ref[...].astype(bf16)
    for part in range(4):
        if part < 3:
            piece = dg(h, delta[part * channels : (part + 1) * channels, :], 0, 1)
        else:
            piece = dg(att, g, 1, 0)
        sums_ref[part * channels : (part + 1) * channels, :] = piece.astype(bf16)


def forward_kernel(group, cap, me_ref, qkv_ref, *rest):
    feats_refs = rest[0:group]
    h_ref, proj, powers_ref, att_ref, inv_ref, spots_ref = rest[group:]
    n, channels = h_ref.shape
    size = channels // HEADS
    h = jnp.zeros((n, channels), f32)
    for s in range(group):
        spot = spots_of(feats_refs[s], cap)
        spots_ref[s] = spot
        h = h + dg(place_matrix(spot, n), feats_refs[s][0:cap, :], 1, 0)
    h = h.astype(bf16)
    h_ref[...] = h
    proj[...] = dg(qkv_ref[0], h, 0, 1).astype(bf16)
    loop_heads(
        HEADS,
        2,
        lambda heads: forward_heads(heads, channels, size, proj, powers_ref, att_ref, inv_ref),
    )


def backward_kernel(group, cap, blocks, me_ref, out_ref, h_ref, proj, powers_ref, att_ref, inv_ref, spots_ref, late_ref, *rest):
    grads_refs = rest[0:group]
    delta, keep_ref, send_ref = rest[group : group + 3]
    out_delta = rest[group + 3]
    n, channels = h_ref.shape
    size = channels // HEADS
    g = jnp.zeros((n, channels), f32)
    for s in range(group):
        g = g + dg(place_matrix(spots_ref[s], n), grads_refs[s][...], 1, 0)
    g = g.astype(bf16)
    out_delta[...] = dg(out_ref[0], g, 1, 1).astype(bf16)
    loop_heads(
        HEADS,
        2,
        lambda heads: backward_heads(
            heads, channels, size, proj, out_delta, powers_ref, att_ref, inv_ref, delta
        ),
    )
    me = me_ref[0]
    h = h_ref[...]
    att = att_ref[...].astype(bf16)
    rows = 4 * channels // blocks
    half = blocks // 2
    for part in range(4):
        if part < 3:
            piece = dg(h, delta[part * channels : (part + 1) * channels, :], 0, 1)
        else:
            piece = dg(att, g, 1, 0)
        piece = piece.astype(bf16)
        for c in range(part * blocks // 4, (part + 1) * blocks // 4):
            first = c * rows - part * channels
            block = c ^ me
            both = (piece[first : first + rows, :], late_ref[c * rows : (c + 1) * rows, :])

            @pl.when(block < half)
            def _():
                keep_ref[block % half, 0:rows, :] = both[0]
                keep_ref[block % half, rows : 2 * rows, :] = both[1]

            @pl.when(block >= half)
            def _():
                send_ref[block % half, 0:rows, :] = both[0]
                send_ref[block % half, rows : 2 * rows, :] = both[1]


def rows_kernel(group, cap, me_ref, qkv_ref, delta, spots_ref, *send_refs):
    early = dg(qkv_ref[0], delta[...], 1, 0).T.astype(bf16)
    n = early.shape[0]
    for s in range(group):
        send_refs[s][...] = dg(place_matrix(spots_ref[s], n), early, 0, 0).astype(bf16)


def join_kernel(group, cap, me_ref, slots_ref, mid_ref, *rest):
    back_refs, input_ref = rest[:group], rest[group]
    slots = slots_ref[...]
    total = jnp.zeros(mid_ref.shape, f32)
    for s in range(group):
        total = total + dg(slot_matrix(slots, s * cap, cap), back_refs[s][...], 0, 0)
    input_ref[...] = (mid_ref[...].astype(f32) + total.astype(bf16).astype(f32)).astype(bf16)


def tree_sum(values):
    while len(values) > 1:
        values = [values[i] + values[i + 1] for i in range(0, len(values), 2)]
    return values[0]


def add_kernel(count, me_ref, *rest):
    ins, outs = rest[:count], rest[count:]
    m = outs[0].shape[0]
    for j, out in enumerate(outs):
        for b in range(m):
            out[b] = tree_sum([x[j * m + b].astype(f32) for x in ins]).astype(bf16)


def add_parts(me, parts, pieces):
    dims = parts[0].shape
    out = [shape((dims[0] // pieces,) + dims[1:], bf16)] * pieces
    return call(partial(add_kernel, len(parts)), out, [me] + list(parts))


def finish_kernel(scale, me_ref, *rest):
    refs, (qkv_ref, out_ref) = rest[:-2], rest[-2:]
    me = me_ref[0]
    blocks = len(refs)
    _, rows, channels = refs[0].shape
    rows = rows // 2
    for s in range(blocks):
        chunk = s ^ me
        for l in range(2):
            piece = refs[s][0, l * rows : (l + 1) * rows, :].astype(f32) * scale
            part = chunk * rows // channels
            first = pl.multiple_of(chunk * rows % channels, rows)
            for p in range(3):
                @pl.when(part == p)
                def _():
                    qkv_ref[l, pl.ds(first, rows), p * channels : (p + 1) * channels] = piece

            @pl.when(part == 3)
            def _():
                out_ref[l, pl.ds(first, rows), :] = piece


def swap(x, mask, devices):
    return lax.ppermute(x, AXES, [(d, d ^ mask) for d in range(devices)])


def exchange(blocks, devices):
    return [blocks[0]] + [swap(blocks[s], s, devices) for s in range(1, len(blocks))]


def stage_masks(bits):
    masks = [0]
    for b in bits:
        masks = masks + [m | (1 << b) for m in masks]
    return masks


def on_device(section_input, mid_features, out_grad, to_hilbert, to_zorder, qkv_weight, out_weight):
    devices = lax.axis_size("wide") * lax.axis_size("narrow")
    n, channels = section_input.shape
    group = devices // 8
    share = n // group
    cap = share + 2 * (share // 4)
    rank = (lax.axis_index("wide") * lax.axis_size("narrow") + lax.axis_index("narrow")).astype(i32)
    me = rank.reshape(1)
    blocks = 8
    low = rank % blocks
    place = ((low & 1) << 2 | (low >> 1)).reshape(1)
    bits = devices.bit_length() - 1
    whole_stages = [tuple(range(b, min(b + 2, bits))) for b in range(3, bits, 2)]

    size_rows = shape((n, channels), bf16)
    size_send = shape((cap, channels), bf16)
    powers_s, att_s, inv_s = (HEADS, n, n), (channels, n), (HEADS, n)
    chunk = (2 * 4 * channels // blocks, channels)

    slots, *feats = call(
        partial(route_kernel, group, cap),
        [shape((1, n), i32)] + [shape((cap + 16, channels), bf16)] * group,
        [me, to_zorder.reshape(1, n), section_input],
    )
    feats = exchange(feats, devices)
    mid, late_sums, *grads = call(
        partial(late_kernel, group, cap),
        [size_rows, shape((4 * channels, channels), bf16)] + [size_send] * group,
        [me, mid_features, out_grad, qkv_weight, out_weight, slots],
        [
            pltpu.VMEM((4 * channels, n), bf16),
            pltpu.VMEM((3 * channels, n), bf16),
            pltpu.VMEM(powers_s, bf16),
            pltpu.VMEM(att_s, f32),
            pltpu.VMEM(inv_s, f32),
        ],
        us=18,
    )
    grads = exchange(grads, devices)
    h, proj, powers, att, inv, spots = call(
        partial(forward_kernel, group, cap),
        [
            size_rows,
            shape((3 * channels, n), bf16),
            shape(powers_s, bf16),
            shape(att_s, f32),
            shape(inv_s, f32),
            shape((group, 1, cap), i32),
        ],
        [me, qkv_weight, *feats],
        us=8,
    )
    delta, keep, send = call(
        partial(backward_kernel, group, cap, blocks),
        [
            shape((3 * channels, n), bf16),
            shape((blocks // 2,) + chunk, bf16),
            shape((blocks // 2,) + chunk, bf16),
        ],
        [place, out_weight, h, proj, powers, att, inv, spots, late_sums, *grads],
        [pltpu.VMEM((channels, n), bf16)],
        us=10,
    )
    got = swap(send, 1, devices)
    backs = call(
        partial(rows_kernel, group, cap),
        [size_send] * group,
        [me, qkv_weight, delta, spots],
        us=2,
    )
    pieces = add_parts(me, [keep, got], 4)
    masks = stage_masks((1, 2))
    parts = [pieces[0]] + [swap(pieces[i], masks[i], devices) for i in range(1, 4)]
    (total,) = add_parts(me, parts, 1)
    backs = exchange(backs, devices)
    for stage in whole_stages:
        parts = [total] + [swap(total, m, devices) for m in stage_masks(stage)[1:]]
        (total,) = add_parts(me, parts, 1)
    parts = [total] + [swap(total, m, devices) for m in masks[1:]]
    parts = parts + [swap(x, 1, devices) for x in parts]
    (input_grad,) = call(
        partial(join_kernel, group, cap), [size_rows], [me, slots, mid, *backs]
    )
    qkv_grad, out_w_grad = call(
        partial(finish_kernel, float((n * devices) ** -0.5)),
        [shape(qkv_weight.shape, f32), shape(out_weight.shape, f32)],
        [place, *parts],
    )
    return (input_grad, qkv_grad, out_w_grad)


def solution(mesh):
    placed = (
        P(AXES, None),
        P(AXES, None),
        P(AXES, None),
        P(AXES),
        P(AXES),
        P(),
        P(),
    )
    return jax.shard_map(
        on_device,
        mesh=mesh,
        in_specs=placed,
        out_specs=(P(AXES, None), P(), P()),
        check_vma=False,
    )
```

```python
from functools import partial

import jax
import jax.numpy as jnp
from jax import lax
from jax.experimental import pallas as pl
from jax.experimental.pallas import tpu as pltpu
from jax.sharding import PartitionSpec as P

HEADS = 16
LOG2E = 1.4426950408889634
f32, bf16, i32 = jnp.float32, jnp.bfloat16, jnp.int32
AXES = ("wide", "narrow")
VMEM_LIMIT = 40 * 2**20
TOGETHER = 4


def shape(dims, dtype):
    return jax.ShapeDtypeStruct(tuple(dims), dtype)


def dg(a, b, contract_a, contract_b):
    return lax.dot_general(
        a, b, (((contract_a,), (contract_b,)), ((), ())), preferred_element_type=f32
    )


def call(body, out_shape, args, scratch=(), us=1, in_hbm=0):
    args = list(args)
    for i in range(len(args) - in_hbm, len(args)):
        args[i] = pltpu.with_memory_space_constraint(args[i], pltpu.HBM)
    return pl.pallas_call(
        body,
        out_shape=tuple(out_shape),
        in_specs=[pl.BlockSpec(memory_space=pltpu.SMEM)]
        + [pl.BlockSpec(memory_space=pltpu.VMEM)] * (len(args) - 1 - in_hbm)
        + [pl.BlockSpec(memory_space=pltpu.HBM)] * in_hbm,
        out_specs=tuple([pl.BlockSpec(memory_space=pltpu.VMEM)] * len(out_shape)),
        scratch_shapes=list(scratch),
        compiler_params=pltpu.CompilerParams(vmem_limit_bytes=VMEM_LIMIT),
        cost_estimate=pl.CostEstimate(flops=us * 10**9, bytes_accessed=2**20, transcendentals=0),
    )(*args)


def slot_matrix(slots, first, count):
    rows = slots.shape[1]
    at = lax.broadcasted_iota(i32, (count, rows), 0) + first
    return (at == slots).astype(f32).astype(bf16)


def place_matrix(spot, n):
    at = lax.broadcasted_iota(i32, (n, spot.shape[1]), 0)
    return (at == spot).astype(f32).astype(bf16)


def spots_of(recv_ref, cap):
    info = recv_ref[cap : cap + 16, 0:cap].astype(f32)
    spot = info[0:1] + 256.0 * info[1:2] + 1024.0 * (info[2:3] - 1.0)
    return spot.astype(i32)


def route_kernel(group, cap, me_ref, tz_hbm, rows_hbm, h_hbm, g_hbm, qkv_hbm, out_hbm, *rest):
    slots_ref, send_refs = rest[0], rest[1 : 1 + group]
    tz_ref, rows_ref, sems = rest[5 + group :]
    sources = (tz_hbm, rows_hbm, h_hbm, g_hbm, qkv_hbm, out_hbm)
    targets = (tz_ref, rows_ref) + tuple(rest[1 + group : 5 + group])
    copies = [
        pltpu.make_async_copy(a, b, sems.at[i]) for i, (a, b) in enumerate(zip(sources, targets))
    ]
    for copy in copies:
        copy.start()
    copies[0].wait()
    copies[1].wait()
    n, channels = rows_ref.shape
    here = me_ref[0] % group
    target = tz_ref[...]
    partner = (target // n % group) ^ here
    spot = target % n
    lanes = max(16, group)
    which = lax.broadcasted_iota(i32, (lanes, n), 0)
    mine = (which == partner).astype(f32)
    earlier = (
        lax.broadcasted_iota(i32, (n, n), 0) < lax.broadcasted_iota(i32, (n, n), 1)
    ).astype(f32).astype(bf16)
    before = dg(mine.astype(bf16), earlier, 1, 0)
    rank = jnp.sum(mine * before, axis=0, keepdims=True).astype(i32)
    slots = partner * cap + rank
    slots_ref[...] = slots
    row_at = lax.broadcasted_iota(i32, (16, n), 0)
    info = jnp.where(
        row_at == 0, spot % 256, jnp.where(row_at == 1, spot // 256, (row_at == 2).astype(i32))
    ).astype(f32).astype(bf16)
    rows = rows_ref[...]
    for s in range(group):
        chosen = slot_matrix(slots, s * cap, cap)
        send_refs[s][0:cap, :] = dg(chosen, rows, 1, 0).astype(bf16)
        where = dg(info, chosen, 1, 1)
        if cap < channels:
            where = jnp.concatenate([where, jnp.zeros((16, channels - cap), f32)], axis=1)
        send_refs[s][cap : cap + 16, :] = where.astype(bf16)
    for copy in copies[2:]:
        copy.wait()


def two_terms(x):
    high = x.astype(bf16)
    return jnp.concatenate([high, (x - high.astype(f32)).astype(bf16)], axis=0)


def forward_heads(heads, kept, channels, size, proj, powers_ref, att_ref, inv_ref):
    every = range(len(heads))
    at = [pl.multiple_of(h * size, size) for h in heads]
    q = [proj[pl.ds(r, size), :] for r in at]
    k = [proj[pl.ds(channels + r, size), :] for r in at]
    v = [proj[pl.ds(2 * channels + r, size), :] for r in at]
    k = [jnp.concatenate([x, x], axis=0) for x in k]
    q = [two_terms(x.astype(f32) * (size**-0.5 * LOG2E)) for x in q]
    scores = [dg(k[i], q[i], 0, 0) for i in every]
    peaks = [jnp.max(x, axis=0, keepdims=True) for x in scores]
    powers = [jnp.exp2(scores[i] - peaks[i]) for i in every]
    half = [x.astype(bf16) for x in powers]
    inverse = [1.0 / jnp.sum(x, axis=0, keepdims=True) for x in powers]
    attended = [dg(v[i], half[i], 1, 0) * inverse[i] for i in every]
    for i in every:
        powers_ref[kept[i]] = half[i]
        inv_ref[pl.ds(heads[i], 1), :] = inverse[i]
        att_ref[pl.ds(at[i], size), :] = attended[i]


def backward_heads(
    heads, kept, channels, size, proj, out_delta, powers_ref, att_ref, inv_ref, delta, turned_ref
):
    every = range(len(heads))
    at = [pl.multiple_of(h * size, size) for h in heads]
    q = [proj[pl.ds(r, size), :] for r in at]
    k = [proj[pl.ds(channels + r, size), :] for r in at]
    v = [proj[pl.ds(2 * channels + r, size), :] for r in at]
    o = [out_delta[pl.ds(r, size), :].astype(f32) for r in at]
    inverse = [inv_ref[pl.ds(h, 1), :] for h in heads]
    half = [powers_ref[x] for x in kept]
    centre = [
        jnp.sum(att_ref[pl.ds(at[i], size), :] * o[i], axis=0, keepdims=True) * inverse[i]
        for i in every
    ]
    o = [two_terms(o[i] * inverse[i]) for i in every]
    v = [jnp.concatenate([x, x], axis=0) for x in v]
    score_grad = [
        (half[i].astype(f32) * (dg(v[i], o[i], 0, 0) - centre[i])).astype(bf16) for i in every
    ]
    for i in every:
        turned_ref[0, i] = half[i].T
    value = [dg(o[i], turned_ref[0, i], 1, 0) for i in every]
    query = [dg(k[i], score_grad[i], 1, 0) for i in every]
    for i in every:
        turned_ref[1, i] = score_grad[i].T
    key = [dg(q[i], turned_ref[1, i], 1, 0) for i in every]
    scale = size**-0.5
    for i in every:
        delta[pl.ds(at[i], size), :] = (query[i] * scale).astype(bf16)
        delta[pl.ds(channels + at[i], size), :] = (key[i] * scale).astype(bf16)
        delta[pl.ds(2 * channels + at[i], size), :] = (value[i][0:size] + value[i][size:]).astype(bf16)


def loop_heads(body):
    def step(i, carry):
        body([i * TOGETHER + u for u in range(TOGETHER)])
        return carry

    lax.fori_loop(0, HEADS // TOGETHER, step, 0)


def late_kernel(group, cap, me_ref, h_ref, g_ref, qkv_ref, out_ref, slots_ref, *rest):
    mid_ref, sums_ref = rest[0], rest[1]
    send_refs = rest[2 : 2 + group]
    proj, delta, powers_ref, att_ref, inv_ref, turned_ref = rest[2 + group :]
    h, g = h_ref[...], g_ref[...]
    n, channels = h.shape
    size = channels // HEADS
    qkv_w = qkv_ref[1]
    proj[0 : 3 * channels, :] = dg(qkv_w, h, 0, 1).astype(bf16)
    proj[3 * channels : 4 * channels, :] = dg(out_ref[1], g, 1, 1).astype(bf16)
    out_delta = proj.at[3 * channels : 4 * channels, :]

    def body(heads):
        kept = range(TOGETHER)
        forward_heads(heads, kept, channels, size, proj, powers_ref, att_ref, inv_ref)
        backward_heads(
            heads,
            kept,
            channels,
            size,
            proj,
            out_delta,
            powers_ref,
            att_ref,
            inv_ref,
            delta,
            turned_ref,
        )

    loop_heads(body)
    qkv_delta = delta[...]
    row_grad = dg(qkv_w, qkv_delta, 1, 0).T
    mid = (g.astype(f32) + row_grad).astype(bf16)
    mid_ref[...] = mid
    slots = slots_ref[...]
    for s in range(group):
        send_refs[s][...] = dg(slot_matrix(slots, s * cap, cap), mid, 1, 0).astype(bf16)
    att = att_ref[...].astype(bf16)
    for part in range(4):
        if part < 3:
            piece = dg(h, delta[part * channels : (part + 1) * channels, :], 0, 1)
        else:
            piece = dg(att, g, 1, 0)
        sums_ref[part * channels : (part + 1) * channels, :] = piece.astype(bf16)


def forward_kernel(group, cap, me_ref, qkv_ref, *rest):
    feats_refs = rest[0:group]
    h_ref, proj, powers_ref, att_ref, inv_ref, spots_ref = rest[group:]
    n, channels = h_ref.shape
    size = channels // HEADS
    h = jnp.zeros((n, channels), f32)
    for s in range(group):
        spot = spots_of(feats_refs[s], cap)
        spots_ref[s] = spot
        h = h + dg(place_matrix(spot, n), feats_refs[s][0:cap, :], 1, 0)
    h = h.astype(bf16)
    h_ref[...] = h
    proj[...] = dg(qkv_ref[0], h, 0, 1).astype(bf16)
    loop_heads(
        lambda heads: forward_heads(
            heads, heads, channels, size, proj, powers_ref, att_ref, inv_ref
        )
    )


def backward_kernel(group, cap, blocks, me_ref, out_ref, h_ref, proj, powers_ref, att_ref, inv_ref, spots_ref, late_ref, *rest):
    grads_refs = rest[0:group]
    delta, keep_ref, send_ref = rest[group : group + 3]
    out_delta, turned_ref = rest[group + 3 :]
    n, channels = h_ref.shape
    size = channels // HEADS
    g = jnp.zeros((n, channels), f32)
    for s in range(group):
        g = g + dg(place_matrix(spots_ref[s], n), grads_refs[s][...], 1, 0)
    g = g.astype(bf16)
    out_delta[...] = dg(out_ref[0], g, 1, 1).astype(bf16)
    loop_heads(
        lambda heads: backward_heads(
            heads,
            heads,
            channels,
            size,
            proj,
            out_delta,
            powers_ref,
            att_ref,
            inv_ref,
            delta,
            turned_ref,
        )
    )
    me = me_ref[0]
    h = h_ref[...]
    att = att_ref[...].astype(bf16)
    rows = 4 * channels // blocks
    half = blocks // 2
    for part in range(4):
        if part < 3:
            piece = dg(h, delta[part * channels : (part + 1) * channels, :], 0, 1)
        else:
            piece = dg(att, g, 1, 0)
        piece = piece.astype(bf16)
        for c in range(part * blocks // 4, (part + 1) * blocks // 4):
            first = c * rows - part * channels
            block = c ^ me
            both = (piece[first : first + rows, :], late_ref[c * rows : (c + 1) * rows, :])

            @pl.when(block < half)
            def _():
                keep_ref[block % half, 0:rows, :] = both[0]
                keep_ref[block % half, rows : 2 * rows, :] = both[1]

            @pl.when(block >= half)
            def _():
                send_ref[block % half, 0:rows, :] = both[0]
                send_ref[block % half, rows : 2 * rows, :] = both[1]


def rows_kernel(group, cap, me_ref, qkv_ref, delta, spots_ref, *send_refs):
    early = dg(qkv_ref[0], delta[...], 1, 0).T.astype(bf16)
    n = early.shape[0]
    for s in range(group):
        send_refs[s][...] = dg(place_matrix(spots_ref[s], n), early, 0, 0).astype(bf16)


def join_kernel(group, cap, me_ref, slots_ref, mid_ref, *rest):
    back_refs, input_ref = rest[:group], rest[group]
    slots = slots_ref[...]
    total = jnp.zeros(mid_ref.shape, f32)
    for s in range(group):
        total = total + dg(slot_matrix(slots, s * cap, cap), back_refs[s][...], 0, 0)
    input_ref[...] = (mid_ref[...].astype(f32) + total.astype(bf16).astype(f32)).astype(bf16)


def tree_sum(values):
    while len(values) > 1:
        values = [values[i] + values[i + 1] for i in range(0, len(values), 2)]
    return values[0]


def add_kernel(count, me_ref, *rest):
    ins, outs = rest[:count], rest[count:]
    m = outs[0].shape[0]
    for j, out in enumerate(outs):
        for b in range(m):
            out[b] = tree_sum([x[j * m + b].astype(f32) for x in ins]).astype(bf16)


def add_parts(me, parts, pieces):
    dims = parts[0].shape
    out = [shape((dims[0] // pieces,) + dims[1:], bf16)] * pieces
    return call(partial(add_kernel, len(parts)), out, [me] + list(parts))


def finish_kernel(scale, me_ref, *rest):
    refs, (qkv_ref, out_ref) = rest[:-2], rest[-2:]
    me = me_ref[0]
    blocks = len(refs)
    _, rows, channels = refs[0].shape
    rows = rows // 2
    for s in range(blocks):
        chunk = s ^ me
        for l in range(2):
            piece = refs[s][0, l * rows : (l + 1) * rows, :].astype(f32) * scale
            part = chunk * rows // channels
            first = pl.multiple_of(chunk * rows % channels, rows)
            for p in range(3):
                @pl.when(part == p)
                def _():
                    qkv_ref[l, pl.ds(first, rows), p * channels : (p + 1) * channels] = piece

            @pl.when(part == 3)
            def _():
                out_ref[l, pl.ds(first, rows), :] = piece


def swap(x, mask, devices):
    return lax.ppermute(x, AXES, [(d, d ^ mask) for d in range(devices)])


def exchange(blocks, devices):
    return [blocks[0]] + [swap(blocks[s], s, devices) for s in range(1, len(blocks))]


def stage_masks(bits):
    masks = [0]
    for b in bits:
        masks = masks + [m | (1 << b) for m in masks]
    return masks


def on_device(section_input, mid_features, out_grad, to_hilbert, to_zorder, qkv_weight, out_weight):
    devices = lax.axis_size("wide") * lax.axis_size("narrow")
    n, channels = section_input.shape
    group = devices // 8
    share = n // group
    cap = share + 2 * (share // 4)
    rank = (lax.axis_index("wide") * lax.axis_size("narrow") + lax.axis_index("narrow")).astype(i32)
    me = rank.reshape(1)
    blocks = 8
    low = rank % blocks
    place = ((low & 1) << 2 | (low >> 1)).reshape(1)
    bits = devices.bit_length() - 1
    whole_stages = [tuple(range(b, min(b + 2, bits))) for b in range(3, bits, 2)]

    size_rows = shape((n, channels), bf16)
    size_send = shape((cap, channels), bf16)
    turned = pltpu.VMEM((2, TOGETHER, n, n), bf16)
    powers_s, att_s, inv_s = (HEADS, n, n), (channels, n), (HEADS, n)
    chunk = (2 * 4 * channels // blocks, channels)

    moved = [mid_features, out_grad, qkv_weight, out_weight]
    slots, *rest = call(
        partial(route_kernel, group, cap),
        [shape((1, n), i32)]
        + [shape((cap + 16, channels), bf16)] * group
        + [shape(x.shape, bf16) for x in moved],
        [me, to_zorder.reshape(1, n), section_input] + moved,
        [
            pltpu.VMEM((1, n), i32),
            pltpu.VMEM((n, channels), bf16),
            pltpu.SemaphoreType.DMA((6,)),
        ],
        us=2,
        in_hbm=6,
    )
    feats = exchange(rest[:group], devices)
    mid_features, out_grad, qkv_w, out_w = rest[group:]
    mid, late_sums, *grads = call(
        partial(late_kernel, group, cap),
        [size_rows, shape((4 * channels, channels), bf16)] + [size_send] * group,
        [me, mid_features, out_grad, qkv_w, out_w, slots],
        [
            pltpu.VMEM((4 * channels, n), bf16),
            pltpu.VMEM((3 * channels, n), bf16),
            pltpu.VMEM((TOGETHER, n, n), bf16),
            pltpu.VMEM(att_s, f32),
            pltpu.VMEM(inv_s, f32),
            turned,
        ],
        us=16,
    )
    grads = exchange(grads, devices)
    h, proj, powers, att, inv, spots = call(
        partial(forward_kernel, group, cap),
        [
            size_rows,
            shape((3 * channels, n), bf16),
            shape(powers_s, bf16),
            shape(att_s, f32),
            shape(inv_s, f32),
            shape((group, 1, cap), i32),
        ],
        [me, qkv_w, *feats],
        us=8,
    )
    delta, keep, send = call(
        partial(backward_kernel, group, cap, blocks),
        [
            shape((3 * channels, n), bf16),
            shape((blocks // 2,) + chunk, bf16),
            shape((blocks // 2,) + chunk, bf16),
        ],
        [place, out_w, h, proj, powers, att, inv, spots, late_sums, *grads],
        [pltpu.VMEM((channels, n), bf16), turned],
        us=9,
    )
    got = swap(send, 1, devices)
    backs = call(
        partial(rows_kernel, group, cap),
        [size_send] * group,
        [me, qkv_w, delta, spots],
        us=2,
    )
    pieces = add_parts(me, [keep, got], 4)
    masks = stage_masks((1, 2))
    parts = [pieces[0]] + [swap(pieces[i], masks[i], devices) for i in range(1, 4)]
    (total,) = add_parts(me, parts, 1)
    backs = exchange(backs, devices)
    for stage in whole_stages:
        parts = [total] + [swap(total, m, devices) for m in stage_masks(stage)[1:]]
        (total,) = add_parts(me, parts, 1)
    (input_grad,) = call(
        partial(join_kernel, group, cap), [size_rows], [me, slots, mid, *backs]
    )
    total, input_grad = lax.optimization_barrier((total, input_grad))
    parts = [total] + [swap(total, m, devices) for m in masks[1:]]
    parts = parts + [swap(x, 1, devices) for x in parts]
    qkv_grad, out_w_grad = call(
        partial(finish_kernel, float((n * devices) ** -0.5)),
        [shape(qkv_weight.shape, f32), shape(out_weight.shape, f32)],
        [place, *parts],
    )
    return (input_grad, qkv_grad, out_w_grad)


def solution(mesh):
    placed = (
        P(AXES, None),
        P(AXES, None),
        P(AXES, None),
        P(AXES),
        P(AXES),
        P(),
        P(),
    )
    return jax.shard_map(
        on_device,
        mesh=mesh,
        in_specs=placed,
        out_specs=(P(AXES, None), P(), P()),
        check_vma=False,
    )
```

```python
from functools import partial

import jax
import jax.numpy as jnp
from jax import lax
from jax.experimental import pallas as pl
from jax.experimental.pallas import tpu as pltpu
from jax.sharding import PartitionSpec as P

HEADS = 16
LOG2E = 1.4426950408889634
f32, bf16, i32 = jnp.float32, jnp.bfloat16, jnp.int32
AXES = ("wide", "narrow")
VMEM_LIMIT = 26 * 2**20
KEPT = 4


def shape(dims, dtype):
    return jax.ShapeDtypeStruct(tuple(dims), dtype)


def dg(a, b, contract_a, contract_b):
    return lax.dot_general(
        a, b, (((contract_a,), (contract_b,)), ((), ())), preferred_element_type=f32
    )


def call(body, out_shape, args, scratch=(), us=1, in_hbm=0, out=pltpu.VMEM):
    args = list(args)
    for i in range(len(args) - in_hbm, len(args)):
        args[i] = pltpu.with_memory_space_constraint(args[i], pltpu.HBM)
    return pl.pallas_call(
        body,
        out_shape=tuple(out_shape),
        in_specs=[pl.BlockSpec(memory_space=pltpu.SMEM)]
        + [pl.BlockSpec(memory_space=pltpu.VMEM)] * (len(args) - 1 - in_hbm)
        + [pl.BlockSpec(memory_space=pltpu.HBM)] * in_hbm,
        out_specs=tuple([pl.BlockSpec(memory_space=out)] * len(out_shape)),
        scratch_shapes=list(scratch),
        compiler_params=pltpu.CompilerParams(vmem_limit_bytes=VMEM_LIMIT),
        cost_estimate=pl.CostEstimate(flops=us * 10**9, bytes_accessed=2**20, transcendentals=0),
    )(*args)


def slot_matrix(slots, first, count):
    rows = slots.shape[1]
    at = lax.broadcasted_iota(i32, (count, rows), 0) + first
    return (at == slots).astype(f32).astype(bf16)


def place_matrix(spot, n):
    at = lax.broadcasted_iota(i32, (n, spot.shape[1]), 0)
    return (at == spot).astype(f32).astype(bf16)


def spots_of(recv_ref, cap):
    info = recv_ref[cap : cap + 16, 0:cap].astype(f32)
    spot = info[0:1] + 256.0 * info[1:2] + 1024.0 * (info[2:3] - 1.0)
    return spot.astype(i32)


def route_kernel(group, cap, me_ref, tz_hbm, rows_hbm, h_hbm, g_hbm, qkv_hbm, out_hbm, *rest):
    slots_ref, send_refs = rest[0], rest[1 : 1 + group]
    tz_ref, rows_ref, sems = rest[5 + group :]
    sources = (tz_hbm, rows_hbm, h_hbm, g_hbm, qkv_hbm, out_hbm)
    targets = (tz_ref, rows_ref) + tuple(rest[1 + group : 5 + group])
    copies = [
        pltpu.make_async_copy(a, b, sems.at[i]) for i, (a, b) in enumerate(zip(sources, targets))
    ]
    for copy in copies:
        copy.start()
    copies[0].wait()
    copies[1].wait()
    n, channels = rows_ref.shape
    here = me_ref[0] % group
    target = tz_ref[...]
    partner = (target // n % group) ^ here
    spot = target % n
    lanes = max(16, group)
    which = lax.broadcasted_iota(i32, (lanes, n), 0)
    mine = (which == partner).astype(f32)
    earlier = (
        lax.broadcasted_iota(i32, (n, n), 0) < lax.broadcasted_iota(i32, (n, n), 1)
    ).astype(f32).astype(bf16)
    before = dg(mine.astype(bf16), earlier, 1, 0)
    rank = jnp.sum(mine * before, axis=0, keepdims=True).astype(i32)
    slots = partner * cap + rank
    slots_ref[...] = slots
    row_at = lax.broadcasted_iota(i32, (16, n), 0)
    info = jnp.where(
        row_at == 0, spot % 256, jnp.where(row_at == 1, spot // 256, (row_at == 2).astype(i32))
    ).astype(f32).astype(bf16)
    rows = rows_ref[...]
    for s in range(group):
        chosen = slot_matrix(slots, s * cap, cap)
        send_refs[s][0:cap, :] = dg(chosen, rows, 1, 0).astype(bf16)
        where = dg(info, chosen, 1, 1)
        if cap < channels:
            where = jnp.concatenate([where, jnp.zeros((16, channels - cap), f32)], axis=1)
        send_refs[s][cap : cap + 16, :] = where.astype(bf16)
    for copy in copies[2:]:
        copy.wait()


def two_terms(x):
    high = x.astype(bf16)
    return jnp.concatenate([high, (x - high.astype(f32)).astype(bf16)], axis=0)


class Heads:

    def __init__(self, channels, proj, out_delta, delta, powers, turned, att, inv, grads, turned_grads):
        self.channels, self.size = channels, channels // HEADS
        self.proj, self.out_delta, self.delta = proj, out_delta, delta
        self.powers, self.turned, self.att, self.inv = powers, turned, att, inv
        self.grads, self.turned_grads = grads, turned_grads
        self.held = {}

    def rows(self, ref, part, head):
        first = part * self.channels + head * self.size
        return ref[first : first + self.size, :]

    def scores(self, head):
        k = self.rows(self.proj, 1, head)
        q = self.rows(self.proj, 0, head).astype(f32) * (self.size**-0.5 * LOG2E)
        self.held["s", head] = dg(jnp.concatenate([k, k], axis=0), two_terms(q), 0, 0)

    def softmax(self, head):
        scores = self.held.pop(("s", head))
        powers = jnp.exp2(scores - jnp.max(scores, axis=0, keepdims=True))
        self.powers[head % self.powers.shape[0]] = powers.astype(bf16)
        self.inv[head : head + 1, :] = 1.0 / jnp.sum(powers, axis=0, keepdims=True)

    def attend(self, head):
        slot = head % self.powers.shape[0]
        powers = self.powers[slot]
        first = head * self.size
        self.att[first : first + self.size, :] = (
            dg(self.rows(self.proj, 2, head), powers, 1, 0) * self.inv[head : head + 1, :]
        )
        self.turned[slot] = powers.T

    def prob_grad(self, head):
        o = self.rows(self.out_delta, 0, head).astype(f32)
        inverse = self.inv[head : head + 1, :]
        centre = jnp.sum(self.rows(self.att, 0, head) * o, axis=0, keepdims=True) * inverse
        v = self.rows(self.proj, 2, head)
        o = two_terms(o * inverse)
        self.held["p", head] = dg(jnp.concatenate([v, v], axis=0), o, 0, 0) - centre
        self.held["o", head] = o

    def score_grad(self, head):
        slot = head % self.grads.shape[0]
        powers = self.powers[head % self.powers.shape[0]].astype(f32)
        grad = (powers * self.held.pop(("p", head))).astype(bf16)
        self.grads[slot] = grad
        self.turned_grads[slot] = grad.T

    def products(self, head):
        slot = head % self.grads.shape[0]
        scale = self.size**-0.5
        value = dg(self.held.pop(("o", head)), self.turned[head % self.turned.shape[0]], 1, 0)
        query = dg(self.rows(self.proj, 1, head), self.grads[slot], 1, 0) * scale
        key = dg(self.rows(self.proj, 0, head), self.turned_grads[slot], 1, 0) * scale
        value = value[0 : self.size] + value[self.size :]
        for part, grad in enumerate((query, key, value)):
            first = part * self.channels + head * self.size
            self.delta[first : first + self.size, :] = grad.astype(bf16)


def pipeline(*stages):
    for step in range(HEADS + max(lag for _, lag in stages)):
        for work, lag in stages:
            if 0 <= step - lag < HEADS:
                work(step - lag)


def late_kernel(group, cap, me_ref, h_ref, g_ref, qkv_ref, out_ref, slots_ref, *rest):
    mid_ref, sums_ref = rest[0], rest[1]
    send_refs = rest[2 : 2 + group]
    proj, delta, powers, turned, att_ref, inv_ref, grads, turned_grads = rest[2 + group :]
    h, g = h_ref[...], g_ref[...]
    n, channels = h.shape
    qkv_w = qkv_ref[1]
    proj[0 : 3 * channels, :] = dg(qkv_w, h, 0, 1).astype(bf16)
    proj[3 * channels : 4 * channels, :] = dg(out_ref[1], g, 1, 1).astype(bf16)
    out_delta = proj.at[3 * channels : 4 * channels, :]
    heads = Heads(
        channels, proj, out_delta, delta, powers, turned, att_ref, inv_ref, grads, turned_grads
    )
    pipeline(
        (heads.scores, 0),
        (heads.score_grad, 3),
        (heads.softmax, 1),
        (heads.products, 4),
        (heads.attend, 2),
        (heads.prob_grad, 2),
    )
    qkv_delta = delta[...]
    row_grad = dg(qkv_w, qkv_delta, 1, 0).T
    mid = (g.astype(f32) + row_grad).astype(bf16)
    mid_ref[...] = mid
    slots = slots_ref[...]
    for s in range(group):
        send_refs[s][...] = dg(slot_matrix(slots, s * cap, cap), mid, 1, 0).astype(bf16)
    qkv_grad = dg(h.T, qkv_delta, 1, 1).astype(bf16)
    for part in range(3):
        columns = slice(part * channels, (part + 1) * channels)
        sums_ref[columns, :] = qkv_grad[:, columns]
    sums_ref[3 * channels :, :] = dg(att_ref[...].astype(bf16), g, 1, 0).astype(bf16)


def forward_kernel(group, cap, me_ref, qkv_ref, *rest):
    feats_refs = rest[0:group]
    place_ref, turned_h_ref, proj, powers, turned, att_ref, inv_ref = rest[group:]
    channels, n = turned_h_ref.shape
    for s in range(group):
        place_ref[s] = place_matrix(spots_of(feats_refs[s], cap), n)
    h = sum(dg(place_ref[s], feats_refs[s][0:cap, :], 1, 0) for s in range(group)).astype(bf16)
    turned_h_ref[...] = h.T
    for part in range(3):
        rows = slice(part * channels, (part + 1) * channels)
        proj[rows, :] = dg(qkv_ref[0, :, rows], turned_h_ref[...], 0, 0).astype(bf16)
    heads = Heads(channels, proj, None, None, powers, turned, att_ref, inv_ref, None, None)
    pipeline((heads.softmax, 1), (heads.scores, 0), (heads.attend, 2))


def backward_kernel(group, blocks, me_ref, out_ref, place_ref, turned_h_ref, proj, *rest):
    powers, turned, att_ref, inv_ref, late_ref = rest[0:5]
    grads_refs = rest[5 : 5 + group]
    delta, keep_ref, send_ref, out_delta, grads, turned_grads = rest[5 + group :]
    channels, n = turned_h_ref.shape
    g = sum(dg(place_ref[s], grads_refs[s][...], 1, 0) for s in range(group)).astype(bf16)
    out_delta[...] = dg(out_ref[0], g, 1, 1).astype(bf16)
    heads = Heads(
        channels, proj, out_delta, delta, powers, turned, att_ref, inv_ref, grads, turned_grads
    )
    pipeline((heads.score_grad, 1), (heads.prob_grad, 0), (heads.products, 2))
    me = me_ref[0]
    qkv_grad = dg(turned_h_ref[...], delta[...], 1, 1).astype(bf16)
    out_grad = dg(att_ref[...].astype(bf16), g, 1, 0).astype(bf16)
    rows = 4 * channels // blocks
    half = blocks // 2

    def store(first_ref, second_ref):
        for c in range(blocks):
            ref = first_ref if c < half else second_ref
            part, first = c * rows // channels, c * rows % channels
            if part < 3:
                piece = qkv_grad[first : first + rows, part * channels : (part + 1) * channels]
            else:
                piece = out_grad[first : first + rows, :]
            block = (c ^ me) % half
            ref[block, 0:rows, :] = piece
            ref[block, rows : 2 * rows, :] = late_ref[c * rows : (c + 1) * rows, :]

    @pl.when(me < half)
    def _():
        store(keep_ref, send_ref)

    @pl.when(me >= half)
    def _():
        store(send_ref, keep_ref)


def rows_kernel(group, me_ref, qkv_ref, delta, place_ref, *send_refs):
    early = dg(qkv_ref[0], delta[...], 1, 0).T.astype(bf16)
    for s in range(group):
        send_refs[s][...] = dg(place_ref[s], early, 0, 0).astype(bf16)


def join_kernel(group, cap, me_ref, slots_ref, mid_ref, *rest):
    back_refs, input_ref = rest[:group], rest[group]
    slots = slots_ref[...]
    total = jnp.zeros(mid_ref.shape, f32)
    for s in range(group):
        total = total + dg(slot_matrix(slots, s * cap, cap), back_refs[s][...], 0, 0)
    input_ref[...] = (mid_ref[...].astype(f32) + total.astype(bf16).astype(f32)).astype(bf16)


def tree_sum(values):
    while len(values) > 1:
        values = [values[i] + values[i + 1] for i in range(0, len(values), 2)]
    return values[0]


def add_kernel(count, me_ref, *rest):
    ins, outs = rest[:count], rest[count:]
    m = outs[0].shape[0]
    for j, out in enumerate(outs):
        for b in range(m):
            out[b] = tree_sum([x[j * m + b].astype(f32) for x in ins]).astype(bf16)


def add_parts(me, parts, pieces):
    dims = parts[0].shape
    out = [shape((dims[0] // pieces,) + dims[1:], bf16)] * pieces
    return call(partial(add_kernel, len(parts)), out, [me] + list(parts))


def finish_kernel(scale, me_ref, *rest):
    refs, (qkv_ref, out_ref, ready, sems) = rest[:-4], rest[-4:]
    me = me_ref[0]
    _, rows, channels = refs[0].shape
    rows = rows // 2

    def each(s, l, act):
        chunk = s ^ me
        part = chunk * rows // channels
        first = pl.multiple_of(chunk * rows % channels, rows)

        @pl.when(part < 3)
        def _():
            column = pl.multiple_of(part * channels, channels)
            to = qkv_ref.at[l, pl.ds(first, rows), pl.ds(column, channels)]
            act(pltpu.make_async_copy(ready.at[s, l], to, sems.at[s, l]))

        @pl.when(part == 3)
        def _():
            to = out_ref.at[l, pl.ds(first, rows), :]
            act(pltpu.make_async_copy(ready.at[s, l], to, sems.at[s, l]))

    work = [(s, l) for s in range(len(refs)) for l in range(2)]
    for s, l in work:
        ready[s, l] = refs[s][0, l * rows : (l + 1) * rows, :].astype(f32) * scale
        each(s, l, lambda copy: copy.start())
    for s, l in work:
        each(s, l, lambda copy: copy.wait())


def swap(x, mask, devices):
    return lax.ppermute(x, AXES, [(d, d ^ mask) for d in range(devices)])


def exchange(blocks, devices):
    return [blocks[0]] + [swap(blocks[s], s, devices) for s in range(1, len(blocks))]


def stage_masks(bits):
    masks = [0]
    for b in bits:
        masks = masks + [m | (1 << b) for m in masks]
    return masks


def on_device(section_input, mid_features, out_grad, to_hilbert, to_zorder, qkv_weight, out_weight):
    devices = lax.axis_size("wide") * lax.axis_size("narrow")
    n, channels = section_input.shape
    group = devices // 8
    share = n // group
    cap = share + 2 * (share // 4)
    rank = (lax.axis_index("wide") * lax.axis_size("narrow") + lax.axis_index("narrow")).astype(i32)
    me = rank.reshape(1)
    blocks = 8
    low = rank % blocks
    place = ((low & 1) << 2 | (low >> 1)).reshape(1)
    bits = devices.bit_length() - 1
    whole_stages = [tuple(range(b, min(b + 2, bits))) for b in range(3, bits, 2)]

    size_rows = shape((n, channels), bf16)
    size_send = shape((cap, channels), bf16)
    some_heads = pltpu.VMEM((KEPT, n, n), bf16)
    powers_s, att_s, inv_s = (HEADS, n, n), (channels, n), (HEADS, n)
    chunk = (2 * 4 * channels // blocks, channels)

    moved = [mid_features, out_grad, qkv_weight, out_weight]
    slots, *rest = call(
        partial(route_kernel, group, cap),
        [shape((1, n), i32)]
        + [shape((cap + 16, channels), bf16)] * group
        + [shape(x.shape, bf16) for x in moved],
        [me, to_zorder.reshape(1, n), section_input] + moved,
        [
            pltpu.VMEM((1, n), i32),
            pltpu.VMEM((n, channels), bf16),
            pltpu.SemaphoreType.DMA((6,)),
        ],
        us=2,
        in_hbm=6,
    )
    feats = exchange(rest[:group], devices)
    mid_features, out_grad, qkv_w, out_w = rest[group:]
    mid, late_sums, *grads = call(
        partial(late_kernel, group, cap),
        [size_rows, shape((4 * channels, channels), bf16)] + [size_send] * group,
        [me, mid_features, out_grad, qkv_w, out_w, slots],
        [
            pltpu.VMEM((4 * channels, n), bf16),
            pltpu.VMEM((3 * channels, n), bf16),
            some_heads,
            some_heads,
            pltpu.VMEM(att_s, f32),
            pltpu.VMEM(inv_s, f32),
            some_heads,
            some_heads,
        ],
        us=16,
    )
    grads = exchange(grads, devices)
    place_rows, *layer = call(
        partial(forward_kernel, group, cap),
        [
            shape((group, n, cap), bf16),
            shape((channels, n), bf16),
            shape((3 * channels, n), bf16),
            shape(powers_s, bf16),
            shape(powers_s, bf16),
            shape(att_s, f32),
            shape(inv_s, f32),
        ],
        [me, qkv_w, *feats],
        us=7,
    )
    delta, keep, send = call(
        partial(backward_kernel, group, blocks),
        [
            shape((3 * channels, n), bf16),
            shape((blocks // 2,) + chunk, bf16),
            shape((blocks // 2,) + chunk, bf16),
        ],
        [place, out_w, place_rows, *layer, late_sums, *grads],
        [pltpu.VMEM((channels, n), bf16), some_heads, some_heads],
        us=9,
    )
    got = swap(send, 1, devices)
    backs = call(
        partial(rows_kernel, group),
        [size_send] * group,
        [me, qkv_w, delta, place_rows],
        us=2,
    )
    pieces = add_parts(me, [keep, got], 4)
    masks = stage_masks((1, 2))
    parts = [pieces[0]] + [swap(pieces[i], masks[i], devices) for i in range(1, 4)]
    (total,) = add_parts(me, parts, 1)
    backs = exchange(backs, devices)
    for stage in whole_stages:
        parts = [total] + [swap(total, m, devices) for m in stage_masks(stage)[1:]]
        (total,) = add_parts(me, parts, 1)
    (input_grad,) = call(
        partial(join_kernel, group, cap), [size_rows], [me, slots, mid, *backs]
    )
    total, input_grad = lax.optimization_barrier((total, input_grad))
    parts = [total] + [swap(total, m, devices) for m in masks[1:]]
    parts = parts + [swap(x, 1, devices) for x in parts]
    qkv_grad, out_w_grad = call(
        partial(finish_kernel, float((n * devices) ** -0.5)),
        [shape(qkv_weight.shape, f32), shape(out_weight.shape, f32)],
        [place, *parts],
        [pltpu.VMEM((blocks, 2) + (chunk[0] // 2, channels), f32), pltpu.SemaphoreType.DMA((blocks, 2))],
        out=pltpu.HBM,
    )
    return (input_grad, qkv_grad, out_w_grad)


def solution(mesh):
    placed = (
        P(AXES, None),
        P(AXES, None),
        P(AXES, None),
        P(AXES),
        P(AXES),
        P(),
        P(),
    )
    return jax.shard_map(
        on_device,
        mesh=mesh,
        in_specs=placed,
        out_specs=(P(AXES, None), P(), P()),
        check_vma=False,
    )
```

```python
from functools import partial

import jax
import jax.numpy as jnp
from jax import lax
from jax.experimental import pallas as pl
from jax.experimental.pallas import tpu as pltpu
from jax.sharding import PartitionSpec as P

HEADS = 16
LOG2E = 1.4426950408889634
f32, bf16, i32 = jnp.float32, jnp.bfloat16, jnp.int32
AXES = ("wide", "narrow")
VMEM_LIMIT = 26 * 2**20
KEPT = 4


def shape(dims, dtype):
    return jax.ShapeDtypeStruct(tuple(dims), dtype)


def dg(a, b, contract_a, contract_b):
    return lax.dot_general(
        a, b, (((contract_a,), (contract_b,)), ((), ())), preferred_element_type=f32
    )


def call(body, out_shape, args, scratch=(), us=1, in_hbm=0, out=pltpu.VMEM):
    args = list(args)
    for i in range(len(args) - in_hbm, len(args)):
        args[i] = pltpu.with_memory_space_constraint(args[i], pltpu.HBM)
    return pl.pallas_call(
        body,
        out_shape=tuple(out_shape),
        in_specs=[pl.BlockSpec(memory_space=pltpu.SMEM)]
        + [pl.BlockSpec(memory_space=pltpu.VMEM)] * (len(args) - 1 - in_hbm)
        + [pl.BlockSpec(memory_space=pltpu.HBM)] * in_hbm,
        out_specs=tuple([pl.BlockSpec(memory_space=out)] * len(out_shape)),
        scratch_shapes=list(scratch),
        compiler_params=pltpu.CompilerParams(vmem_limit_bytes=VMEM_LIMIT),
        cost_estimate=pl.CostEstimate(flops=us * 10**9, bytes_accessed=2**20, transcendentals=0),
    )(*args)


def slot_matrix(slots, first, count):
    rows = slots.shape[1]
    at = lax.broadcasted_iota(i32, (count, rows), 0) + first
    return jnp.where(at == slots, 1.0, 0.0).astype(bf16)


def place_matrix(spot, n):
    at = lax.broadcasted_iota(i32, (n, spot.shape[1]), 0)
    return jnp.where(at == spot, 1.0, 0.0).astype(bf16)


def placed_rows(place_ref, blocks):
    rows = jnp.concatenate(blocks, axis=0)
    n = place_ref.shape[0]
    halves = [dg(place_ref[i : i + n // 2, :], rows, 1, 0) for i in (0, n // 2)]
    return jnp.concatenate(halves, axis=0).astype(bf16)


def spots_of(recv_ref, cap):
    info = recv_ref[cap : cap + 16, 0:cap].astype(f32)
    spot = info[0:1] + 256.0 * info[1:2] + 1024.0 * (info[2:3] - 1.0)
    return spot.astype(i32)


def route_kernel(group, cap, me_ref, tz_hbm, rows_hbm, h_hbm, g_hbm, qkv_hbm, out_hbm, *rest):
    slots_ref, send_refs = rest[0], rest[1 : 1 + group]
    tz_ref, rows_ref, sems = rest[5 + group :]
    sources = (tz_hbm, rows_hbm, h_hbm, g_hbm, qkv_hbm, out_hbm)
    targets = (tz_ref, rows_ref) + tuple(rest[1 + group : 5 + group])
    copies = [
        pltpu.make_async_copy(a, b, sems.at[i]) for i, (a, b) in enumerate(zip(sources, targets))
    ]
    for copy in copies:
        copy.start()
    copies[0].wait()
    copies[1].wait()
    n, channels = rows_ref.shape
    here = me_ref[0] % group
    target = tz_ref[...]
    partner = (target // n % group) ^ here
    spot = target % n
    lanes = max(16, group)
    which = lax.broadcasted_iota(i32, (lanes, n), 0)
    mine = jnp.where(which == partner, 1.0, 0.0)
    earlier = jnp.where(
        lax.broadcasted_iota(i32, (n, n), 0) < lax.broadcasted_iota(i32, (n, n), 1), 1.0, 0.0
    ).astype(bf16)
    before = dg(mine.astype(bf16), earlier, 1, 0)
    rank = jnp.sum(mine * before, axis=0, keepdims=True).astype(i32)
    slots = partner * cap + rank
    slots_ref[...] = slots
    row_at = lax.broadcasted_iota(i32, (16, n), 0)
    info = jnp.where(
        row_at == 0, spot % 256, jnp.where(row_at == 1, spot // 256, (row_at == 2).astype(i32))
    ).astype(f32).astype(bf16)
    rows = rows_ref[...]
    for s in range(group):
        chosen = slot_matrix(slots, s * cap, cap)
        send_refs[s][0:cap, :] = dg(chosen, rows, 1, 0).astype(bf16)
        where = dg(info, chosen, 1, 1)
        if cap < channels:
            where = jnp.concatenate([where, jnp.zeros((16, channels - cap), f32)], axis=1)
        send_refs[s][cap : cap + 16, :] = where.astype(bf16)
    for copy in copies[2:]:
        copy.wait()


def two_terms(x):
    high = x.astype(bf16)
    return jnp.concatenate([high, (x - high.astype(f32)).astype(bf16)], axis=0)


class Heads:

    def __init__(self, channels, proj, out_delta, delta, powers, turned, att, inv, grads, turned_grads):
        self.channels, self.size = channels, channels // HEADS
        self.proj, self.out_delta, self.delta = proj, out_delta, delta
        self.powers, self.turned, self.att, self.inv = powers, turned, att, inv
        self.grads, self.turned_grads = grads, turned_grads
        self.held = {}

    def rows(self, ref, part, head):
        first = part * self.channels + head * self.size
        return ref[first : first + self.size, :]

    def scores(self, head):
        k = self.rows(self.proj, 1, head)
        q = self.rows(self.proj, 0, head).astype(f32) * (self.size**-0.5 * LOG2E)
        self.held["s", head] = dg(jnp.concatenate([k, k], axis=0), two_terms(q), 0, 0)

    def softmax(self, head):
        scores = self.held.pop(("s", head))
        powers = jnp.exp2(scores - jnp.max(scores, axis=0, keepdims=True))
        self.powers[head % self.powers.shape[0]] = powers.astype(bf16)
        self.inv[head : head + 1, :] = 1.0 / jnp.sum(powers, axis=0, keepdims=True)

    def attend(self, head):
        slot = head % self.powers.shape[0]
        powers = self.powers[slot]
        first = head * self.size
        self.att[first : first + self.size, :] = (
            dg(self.rows(self.proj, 2, head), powers, 1, 0) * self.inv[head : head + 1, :]
        )
        self.turned[slot] = powers.T

    def prob_grad(self, head):
        o = self.rows(self.out_delta, 0, head).astype(f32)
        inverse = self.inv[head : head + 1, :]
        centre = jnp.sum(self.rows(self.att, 0, head) * o, axis=0, keepdims=True) * inverse
        v = self.rows(self.proj, 2, head)
        o = two_terms(o * inverse)
        self.held["p", head] = dg(jnp.concatenate([v, v], axis=0), o, 0, 0) - centre
        self.held["o", head] = o

    def score_grad(self, head):
        slot = head % self.grads.shape[0]
        powers = self.powers[head % self.powers.shape[0]].astype(f32)
        grad = (powers * self.held.pop(("p", head))).astype(bf16)
        self.grads[slot] = grad
        self.turned_grads[slot] = grad.T

    def products(self, head):
        slot = head % self.grads.shape[0]
        scale = self.size**-0.5
        value = dg(self.held.pop(("o", head)), self.turned[head % self.turned.shape[0]], 1, 0)
        query = dg(self.rows(self.proj, 1, head), self.grads[slot], 1, 0) * scale
        key = dg(self.rows(self.proj, 0, head), self.turned_grads[slot], 1, 0) * scale
        value = value[0 : self.size] + value[self.size :]
        for part, grad in enumerate((query, key, value)):
            first = part * self.channels + head * self.size
            self.delta[first : first + self.size, :] = grad.astype(bf16)


def pipeline(*stages):
    for step in range(HEADS + max(lag for _, lag in stages)):
        for work, lag in stages:
            if 0 <= step - lag < HEADS:
                work(step - lag)


def store_blocks(me, qkv_grad, out_grad, keep_ref, send_ref):
    half, rows, channels = keep_ref.shape

    def store(first_ref, second_ref):
        for c in range(2 * half):
            ref = first_ref if c < half else second_ref
            part, first = c * rows // channels, c * rows % channels
            if part < 3:
                piece = qkv_grad[first : first + rows, part * channels : (part + 1) * channels]
            else:
                piece = out_grad[first : first + rows, :]
            ref[(c ^ me) % half] = piece

    @pl.when(me < half)
    def _():
        store(keep_ref, send_ref)

    @pl.when(me >= half)
    def _():
        store(send_ref, keep_ref)


def late_kernel(group, cap, me_ref, h_ref, g_ref, qkv_ref, out_ref, slots_ref, *rest):
    mid_ref, keep_ref, send_ref = rest[0:3]
    send_refs = rest[3 : 3 + group]
    proj, delta, powers, turned, att_ref, inv_ref, grads, turned_grads = rest[3 + group :]
    h, g = h_ref[...], g_ref[...]
    n, channels = h.shape
    qkv_w = qkv_ref[1]
    proj[0 : 3 * channels, :] = dg(qkv_w, h, 0, 1).astype(bf16)
    proj[3 * channels : 4 * channels, :] = dg(out_ref[1], g, 1, 1).astype(bf16)
    out_delta = proj.at[3 * channels : 4 * channels, :]
    heads = Heads(
        channels, proj, out_delta, delta, powers, turned, att_ref, inv_ref, grads, turned_grads
    )
    pipeline(
        (heads.scores, 0),
        (heads.score_grad, 3),
        (heads.softmax, 1),
        (heads.products, 4),
        (heads.attend, 2),
        (heads.prob_grad, 2),
    )
    qkv_delta = delta[...]
    row_grad = dg(qkv_w, qkv_delta, 1, 0).T
    mid = (g.astype(f32) + row_grad).astype(bf16)
    mid_ref[...] = mid
    slots = slots_ref[...]
    for s in range(group):
        send_refs[s][...] = dg(slot_matrix(slots, s * cap, cap), mid, 1, 0).astype(bf16)
    qkv_grad = dg(h.T, qkv_delta, 1, 1).astype(bf16)
    out_grad = dg(att_ref[...].astype(bf16), g, 1, 0).astype(bf16)
    store_blocks(me_ref[0], qkv_grad, out_grad, keep_ref, send_ref)


def forward_kernel(group, cap, me_ref, qkv_ref, *rest):
    feats_refs = rest[0:group]
    place_ref, turned_h_ref, proj, powers, turned, att_ref, inv_ref = rest[group:]
    channels, n = turned_h_ref.shape
    spots = jnp.concatenate([spots_of(ref, cap) for ref in feats_refs], axis=1)
    place_ref[...] = place_matrix(spots, n)
    h = placed_rows(place_ref, [ref[0:cap, :] for ref in feats_refs])
    turned_h_ref[...] = h.T
    for part in range(3):
        rows = slice(part * channels, (part + 1) * channels)
        proj[rows, :] = dg(qkv_ref[0, :, rows], turned_h_ref[...], 0, 0).astype(bf16)
    heads = Heads(channels, proj, None, None, powers, turned, att_ref, inv_ref, None, None)
    pipeline((heads.softmax, 1), (heads.scores, 0), (heads.attend, 2))


def backward_kernel(group, me_ref, out_ref, place_ref, turned_h_ref, proj, *rest):
    powers, turned, att_ref, inv_ref = rest[0:4]
    grads_refs = rest[4 : 4 + group]
    delta, keep_ref, send_ref, out_delta, grads, turned_grads = rest[4 + group :]
    channels, n = turned_h_ref.shape
    g = placed_rows(place_ref, [ref[...] for ref in grads_refs])
    out_delta[...] = dg(out_ref[0], g, 1, 1).astype(bf16)
    heads = Heads(
        channels, proj, out_delta, delta, powers, turned, att_ref, inv_ref, grads, turned_grads
    )
    pipeline((heads.score_grad, 1), (heads.prob_grad, 0), (heads.products, 2))
    qkv_grad = dg(turned_h_ref[...], delta[...], 1, 1).astype(bf16)
    out_grad = dg(att_ref[...].astype(bf16), g, 1, 0).astype(bf16)
    store_blocks(me_ref[0], qkv_grad, out_grad, keep_ref, send_ref)


def rows_kernel(cap, me_ref, qkv_ref, delta, place_ref, *send_refs):
    early = dg(qkv_ref[0], delta[...], 1, 0).T.astype(bf16)
    rows = dg(place_ref[...], early, 0, 0).astype(bf16)
    for s, ref in enumerate(send_refs):
        ref[...] = rows[s * cap : (s + 1) * cap, :]


def join_kernel(group, cap, me_ref, slots_ref, mid_ref, *rest):
    back_refs, input_ref = rest[:group], rest[group]
    slots = slots_ref[...]
    total = jnp.zeros(mid_ref.shape, f32)
    for s in range(group):
        total = total + dg(slot_matrix(slots, s * cap, cap), back_refs[s][...], 0, 0)
    input_ref[...] = (mid_ref[...].astype(f32) + total.astype(bf16).astype(f32)).astype(bf16)


def tree_sum(values):
    while len(values) > 1:
        values = [values[i] + values[i + 1] for i in range(0, len(values), 2)]
    return values[0]


def add_kernel(counts, me_ref, *rest):
    ins, outs = rest[: sum(counts)], rest[sum(counts) :]
    first = at = 0
    for count in counts:
        group = ins[at : at + count]
        rows = group[0].shape[1]
        for j, out in enumerate(outs):
            out[0, first : first + rows, :] = tree_sum([x[j].astype(f32) for x in group]).astype(bf16)
        first, at = first + rows, at + count


def add_parts(me, groups):
    pieces, _, channels = groups[0][0].shape
    rows = sum(g[0].shape[1] for g in groups)
    return call(
        partial(add_kernel, [len(g) for g in groups]),
        [shape((1, rows, channels), bf16)] * pieces,
        [me] + [x for g in groups for x in g],
    )


def finish_kernel(scale, me_ref, *rest):
    refs, (qkv_ref, out_ref, ready, sems) = rest[:-4], rest[-4:]
    me = me_ref[0]
    _, rows, channels = refs[0].shape
    rows = rows // 2

    def each(s, l, act):
        chunk = s ^ me
        part = chunk * rows // channels
        first = pl.multiple_of(chunk * rows % channels, rows)

        @pl.when(part < 3)
        def _():
            column = pl.multiple_of(part * channels, channels)
            to = qkv_ref.at[l, pl.ds(first, rows), pl.ds(column, channels)]
            act(pltpu.make_async_copy(ready.at[s, l], to, sems.at[s, l]))

        @pl.when(part == 3)
        def _():
            to = out_ref.at[l, pl.ds(first, rows), :]
            act(pltpu.make_async_copy(ready.at[s, l], to, sems.at[s, l]))

    work = [(s, l) for s in range(len(refs)) for l in range(2)]
    for s, l in work:
        ready[s, l] = refs[s][0, l * rows : (l + 1) * rows, :].astype(f32) * scale
        each(s, l, lambda copy: copy.start())
    for s, l in work:
        each(s, l, lambda copy: copy.wait())


def swap(x, mask, devices):
    return lax.ppermute(x, AXES, [(d, d ^ mask) for d in range(devices)])


def exchange(blocks, devices):
    return [blocks[0]] + [swap(blocks[s], s, devices) for s in range(1, len(blocks))]


def stage_masks(bits):
    masks = [0]
    for b in bits:
        masks = masks + [m | (1 << b) for m in masks]
    return masks


def on_device(section_input, mid_features, out_grad, to_hilbert, to_zorder, qkv_weight, out_weight):
    devices = lax.axis_size("wide") * lax.axis_size("narrow")
    n, channels = section_input.shape
    group = devices // 8
    share = n // group
    cap = share + 2 * (share // 4)
    rank = (lax.axis_index("wide") * lax.axis_size("narrow") + lax.axis_index("narrow")).astype(i32)
    me = rank.reshape(1)
    blocks = 8
    low = rank % blocks
    place = ((low & 1) << 2 | (low >> 1)).reshape(1)
    bits = devices.bit_length() - 1
    whole_stages = [tuple(range(b, min(b + 2, bits))) for b in range(3, bits, 2)]

    size_rows = shape((n, channels), bf16)
    size_send = shape((cap, channels), bf16)
    some_heads = pltpu.VMEM((KEPT, n, n), bf16)
    powers_s, att_s, inv_s = (HEADS, n, n), (channels, n), (HEADS, n)
    half = shape((blocks // 2, 4 * channels // blocks, channels), bf16)

    moved = [mid_features, out_grad, qkv_weight, out_weight]
    slots, *rest = call(
        partial(route_kernel, group, cap),
        [shape((1, n), i32)]
        + [shape((cap + 16, channels), bf16)] * group
        + [shape(x.shape, bf16) for x in moved],
        [me, to_zorder.reshape(1, n), section_input] + moved,
        [
            pltpu.VMEM((1, n), i32),
            pltpu.VMEM((n, channels), bf16),
            pltpu.SemaphoreType.DMA((6,)),
        ],
        us=2,
        in_hbm=6,
    )
    feats = exchange(rest[:group], devices)
    mid_features, out_grad, qkv_w, out_w = rest[group:]
    mid, late_keep, late_send, *grads = call(
        partial(late_kernel, group, cap),
        [size_rows, half, half] + [size_send] * group,
        [place, mid_features, out_grad, qkv_w, out_w, slots],
        [
            pltpu.VMEM((4 * channels, n), bf16),
            pltpu.VMEM((3 * channels, n), bf16),
            some_heads,
            some_heads,
            pltpu.VMEM(att_s, f32),
            pltpu.VMEM(inv_s, f32),
            some_heads,
            some_heads,
        ],
        us=16,
    )
    grads = exchange(grads, devices)
    late_got = swap(late_send, 1, devices)
    place_rows, *layer = call(
        partial(forward_kernel, group, cap),
        [
            shape((n, group * cap), bf16),
            shape((channels, n), bf16),
            shape((3 * channels, n), bf16),
            shape(powers_s, bf16),
            shape(powers_s, bf16),
            shape(att_s, f32),
            shape(inv_s, f32),
        ],
        [me, qkv_w, *feats],
        us=7,
    )
    delta, keep, send = call(
        partial(backward_kernel, group),
        [
            shape((3 * channels, n), bf16),
            half,
            half,
        ],
        [place, out_w, place_rows, *layer, *grads],
        [pltpu.VMEM((channels, n), bf16), some_heads, some_heads],
        us=9,
    )
    got = swap(send, 1, devices)
    backs = call(
        partial(rows_kernel, cap),
        [size_send] * group,
        [me, qkv_w, delta, place_rows],
        us=2,
    )
    pieces = add_parts(me, [[keep, got], [late_keep, late_got]])
    masks = stage_masks((1, 2))
    parts = [pieces[0]] + [swap(pieces[i], masks[i], devices) for i in range(1, 4)]
    (total,) = add_parts(me, [parts])
    backs = exchange(backs, devices)
    for stage in whole_stages:
        parts = [total] + [swap(total, m, devices) for m in stage_masks(stage)[1:]]
        (total,) = add_parts(me, [parts])
    (input_grad,) = call(
        partial(join_kernel, group, cap), [size_rows], [me, slots, mid, *backs]
    )
    total, input_grad = lax.optimization_barrier((total, input_grad))
    parts = [total] + [swap(total, m, devices) for m in masks[1:]]
    parts = parts + [swap(x, 1, devices) for x in parts]
    qkv_grad, out_w_grad = call(
        partial(finish_kernel, float((n * devices) ** -0.5)),
        [shape(qkv_weight.shape, f32), shape(out_weight.shape, f32)],
        [place, *parts],
        [
            pltpu.VMEM((blocks, 2) + half.shape[1:], f32),
            pltpu.SemaphoreType.DMA((blocks, 2)),
        ],
        out=pltpu.HBM,
    )
    return (input_grad, qkv_grad, out_w_grad)


def solution(mesh):
    placed = (
        P(AXES, None),
        P(AXES, None),
        P(AXES, None),
        P(AXES),
        P(AXES),
        P(),
        P(),
    )
    return jax.shard_map(
        on_device,
        mesh=mesh,
        in_specs=placed,
        out_specs=(P(AXES, None), P(), P()),
        check_vma=False,
    )
```

```python
from functools import partial

import jax
import jax.numpy as jnp
from jax import lax
from jax.experimental import pallas as pl
from jax.experimental.pallas import tpu as pltpu
from jax.sharding import PartitionSpec as P

HEADS = 16
LOG2E = 1.4426950408889634
f32, bf16, i32 = jnp.float32, jnp.bfloat16, jnp.int32
AXES = ("wide", "narrow")
VMEM_LIMIT = 26 * 2**20
KEPT = 4


def shape(dims, dtype):
    return jax.ShapeDtypeStruct(tuple(dims), dtype)


def dg(a, b, contract_a, contract_b):
    return lax.dot_general(
        a, b, (((contract_a,), (contract_b,)), ((), ())), preferred_element_type=f32
    )


def call(body, out_shape, args, scratch=(), us=1, in_hbm=0, out=pltpu.VMEM):
    args = list(args)
    for i in range(len(args) - in_hbm, len(args)):
        args[i] = pltpu.with_memory_space_constraint(args[i], pltpu.HBM)
    return pl.pallas_call(
        body,
        out_shape=tuple(out_shape),
        in_specs=[pl.BlockSpec(memory_space=pltpu.SMEM)]
        + [pl.BlockSpec(memory_space=pltpu.VMEM)] * (len(args) - 1 - in_hbm)
        + [pl.BlockSpec(memory_space=pltpu.HBM)] * in_hbm,
        out_specs=tuple([pl.BlockSpec(memory_space=out)] * len(out_shape)),
        scratch_shapes=list(scratch),
        compiler_params=pltpu.CompilerParams(vmem_limit_bytes=VMEM_LIMIT),
        cost_estimate=pl.CostEstimate(flops=us * 10**9, bytes_accessed=2**20, transcendentals=0),
    )(*args)


def slot_matrix(slots, first, count):
    rows = slots.shape[1]
    at = lax.broadcasted_iota(i32, (count, rows), 0) + first
    return jnp.where(at == slots, 1.0, 0.0).astype(bf16)


def place_matrix(spot, n):
    at = lax.broadcasted_iota(i32, (n, spot.shape[1]), 0)
    return jnp.where(at == spot, 1.0, 0.0).astype(bf16)


def placed_rows(place_ref, blocks):
    rows = jnp.concatenate(blocks, axis=0)
    n = place_ref.shape[0]
    halves = [dg(place_ref[i : i + n // 2, :], rows, 1, 0) for i in (0, n // 2)]
    return jnp.concatenate(halves, axis=0).astype(bf16)


def spots_of(recv_ref, cap):
    info = recv_ref[cap : cap + 16, 0:cap].astype(f32)
    spot = info[0:1] + 256.0 * info[1:2] + 1024.0 * (info[2:3] - 1.0)
    return spot.astype(i32)


def route_kernel(group, cap, me_ref, tz_hbm, rows_hbm, h_hbm, g_hbm, qkv_hbm, out_hbm, *rest):
    slots_ref, send_refs = rest[0], rest[1 : 1 + group]
    tz_ref, rows_ref, earlier_ref, sems = rest[5 + group :]
    sources = (tz_hbm, rows_hbm, h_hbm, g_hbm, qkv_hbm, out_hbm)
    targets = (tz_ref, rows_ref) + tuple(rest[1 + group : 5 + group])
    copies = [
        pltpu.make_async_copy(a, b, sems.at[i]) for i, (a, b) in enumerate(zip(sources, targets))
    ]
    for copy in copies:
        copy.start()
    n, channels = rows_ref.shape
    earlier_ref[...] = jnp.where(
        lax.broadcasted_iota(i32, (n, n), 0) < lax.broadcasted_iota(i32, (n, n), 1), 1.0, 0.0
    ).astype(bf16)
    copies[0].wait()
    copies[1].wait()
    here = me_ref[0] % group
    target = tz_ref[...]
    partner = (target // n % group) ^ here
    spot = target % n
    lanes = max(16, group)
    which = lax.broadcasted_iota(i32, (lanes, n), 0)
    mine = jnp.where(which == partner, 1.0, 0.0)
    before = dg(mine.astype(bf16), earlier_ref[...], 1, 0)
    rank = jnp.sum(mine * before, axis=0, keepdims=True).astype(i32)
    slots = partner * cap + rank
    slots_ref[...] = slots
    row_at = lax.broadcasted_iota(i32, (16, n), 0)
    info = jnp.where(
        row_at == 0, spot % 256, jnp.where(row_at == 1, spot // 256, (row_at == 2).astype(i32))
    ).astype(f32).astype(bf16)
    rows = rows_ref[...]
    for s in range(group):
        chosen = slot_matrix(slots, s * cap, cap)
        send_refs[s][0:cap, :] = dg(chosen, rows, 1, 0).astype(bf16)
        where = dg(info, chosen, 1, 1)
        if cap < channels:
            where = jnp.concatenate([where, jnp.zeros((16, channels - cap), f32)], axis=1)
        send_refs[s][cap : cap + 16, :] = where.astype(bf16)
    for copy in copies[2:]:
        copy.wait()


def three_terms(x):
    parts = []
    for _ in range(3):
        parts.append(x.astype(bf16))
        x = x - parts[-1].astype(f32)
    return jnp.concatenate(parts, axis=0)


class Heads:

    def __init__(self, channels, proj, out_delta, delta, powers, turned, att, inv, grads, turned_grads):
        self.channels, self.size = channels, channels // HEADS
        self.proj, self.out_delta, self.delta = proj, out_delta, delta
        self.powers, self.turned, self.att, self.inv = powers, turned, att, inv
        self.grads, self.turned_grads = grads, turned_grads
        self.held = {}

    def rows(self, ref, part, head):
        first = part * self.channels + head * self.size
        return ref[first : first + self.size, :]

    def scores(self, head):
        k = self.rows(self.proj, 1, head)
        q = self.rows(self.proj, 0, head).astype(f32) * (self.size**-0.5 * LOG2E)
        self.held["s", head] = dg(jnp.concatenate([k] * 3, axis=0), three_terms(q), 0, 0)

    def softmax(self, head):
        scores = self.held.pop(("s", head))
        powers = jnp.exp2(scores - jnp.max(scores, axis=0, keepdims=True))
        self.powers[head % self.powers.shape[0]] = powers.astype(bf16)
        self.inv[head : head + 1, :] = 1.0 / jnp.sum(powers, axis=0, keepdims=True)

    def attend(self, head):
        slot = head % self.powers.shape[0]
        powers = self.powers[slot]
        first = head * self.size
        self.att[first : first + self.size, :] = (
            dg(self.rows(self.proj, 2, head), powers, 1, 0) * self.inv[head : head + 1, :]
        )
        self.turned[slot] = powers.T

    def prob_grad(self, head):
        o = self.rows(self.out_delta, 0, head).astype(f32)
        inverse = self.inv[head : head + 1, :]
        centre = jnp.sum(self.rows(self.att, 0, head) * o, axis=0, keepdims=True) * inverse
        v = self.rows(self.proj, 2, head)
        o = three_terms(o * inverse)
        self.held["p", head] = dg(jnp.concatenate([v] * 3, axis=0), o, 0, 0) - centre
        self.held["o", head] = o[0 : 2 * self.size]

    def score_grad(self, head):
        slot = head % self.grads.shape[0]
        powers = self.powers[head % self.powers.shape[0]].astype(f32)
        grad = (powers * self.held.pop(("p", head))).astype(bf16)
        self.grads[slot] = grad
        self.turned_grads[slot] = grad.T

    def products(self, head):
        slot = head % self.grads.shape[0]
        scale = self.size**-0.5
        value = dg(self.held.pop(("o", head)), self.turned[head % self.turned.shape[0]], 1, 0)
        query = dg(self.rows(self.proj, 1, head), self.grads[slot], 1, 0) * scale
        key = dg(self.rows(self.proj, 0, head), self.turned_grads[slot], 1, 0) * scale
        value = value[0 : self.size] + value[self.size :]
        for part, grad in enumerate((query, key, value)):
            first = part * self.channels + head * self.size
            self.delta[first : first + self.size, :] = grad.astype(bf16)


def pipeline(*stages):
    for step in range(HEADS + max(lag for _, lag in stages)):
        for work, lag in stages:
            if 0 <= step - lag < HEADS:
                work(step - lag)


def store_blocks(me, qkv_grad, out_grad, keep_ref, send_ref):
    half, rows, channels = keep_ref.shape

    def store(first_ref, second_ref):
        for c in range(2 * half):
            ref = first_ref if c < half else second_ref
            part, first = c * rows // channels, c * rows % channels
            if part < 3:
                piece = qkv_grad[first : first + rows, part * channels : (part + 1) * channels]
            else:
                piece = out_grad[first : first + rows, :]
            ref[(c ^ me) % half] = piece

    @pl.when(me < half)
    def _():
        store(keep_ref, send_ref)

    @pl.when(me >= half)
    def _():
        store(send_ref, keep_ref)


def late_kernel(group, cap, me_ref, h_ref, g_ref, qkv_ref, out_ref, slots_ref, *rest):
    mid_ref, keep_ref, send_ref = rest[0:3]
    send_refs = rest[3 : 3 + group]
    proj, delta, powers, turned, att_ref, inv_ref, grads, turned_grads = rest[3 + group :]
    h, g = h_ref[...], g_ref[...]
    n, channels = h.shape
    qkv_w = qkv_ref[1]
    proj[0 : 3 * channels, :] = dg(qkv_w, h, 0, 1).astype(bf16)
    proj[3 * channels : 4 * channels, :] = dg(out_ref[1], g, 1, 1).astype(bf16)
    out_delta = proj.at[3 * channels : 4 * channels, :]
    heads = Heads(
        channels, proj, out_delta, delta, powers, turned, att_ref, inv_ref, grads, turned_grads
    )
    pipeline(
        (heads.scores, 0),
        (heads.score_grad, 3),
        (heads.softmax, 1),
        (heads.products, 4),
        (heads.attend, 2),
        (heads.prob_grad, 2),
    )
    qkv_delta = delta[...]
    row_grad = dg(qkv_w, qkv_delta, 1, 0).T
    mid = (g.astype(f32) + row_grad).astype(bf16)
    mid_ref[...] = mid
    slots = slots_ref[...]
    for s in range(group):
        send_refs[s][...] = dg(slot_matrix(slots, s * cap, cap), mid, 1, 0).astype(bf16)
    qkv_grad = dg(h.T, qkv_delta, 1, 1).astype(bf16)
    out_grad = dg(att_ref[...].astype(bf16), g, 1, 0).astype(bf16)
    store_blocks(me_ref[0], qkv_grad, out_grad, keep_ref, send_ref)


def forward_kernel(group, cap, me_ref, qkv_ref, *rest):
    feats_refs = rest[0:group]
    place_ref, turned_h_ref, proj, powers, turned, att_ref, inv_ref = rest[group:]
    channels, n = turned_h_ref.shape
    spots = jnp.concatenate([spots_of(ref, cap) for ref in feats_refs], axis=1)
    place_ref[...] = place_matrix(spots, n)
    h = placed_rows(place_ref, [ref[0:cap, :] for ref in feats_refs])
    turned_h_ref[...] = h.T
    for part in range(3):
        rows = slice(part * channels, (part + 1) * channels)
        proj[rows, :] = dg(qkv_ref[0, :, rows], turned_h_ref[...], 0, 0).astype(bf16)
    heads = Heads(channels, proj, None, None, powers, turned, att_ref, inv_ref, None, None)
    pipeline((heads.softmax, 1), (heads.scores, 0), (heads.attend, 2))


def backward_kernel(group, me_ref, out_ref, place_ref, turned_h_ref, proj, *rest):
    powers, turned, att_ref, inv_ref = rest[0:4]
    grads_refs = rest[4 : 4 + group]
    delta, keep_ref, send_ref, out_delta, grads, turned_grads = rest[4 + group :]
    channels, n = turned_h_ref.shape
    g = placed_rows(place_ref, [ref[...] for ref in grads_refs])
    out_delta[...] = dg(out_ref[0], g, 1, 1).astype(bf16)
    heads = Heads(
        channels, proj, out_delta, delta, powers, turned, att_ref, inv_ref, grads, turned_grads
    )
    pipeline((heads.score_grad, 1), (heads.prob_grad, 0), (heads.products, 2))
    qkv_grad = dg(turned_h_ref[...], delta[...], 1, 1).astype(bf16)
    out_grad = dg(att_ref[...].astype(bf16), g, 1, 0).astype(bf16)
    store_blocks(me_ref[0], qkv_grad, out_grad, keep_ref, send_ref)


def rows_kernel(cap, me_ref, qkv_ref, delta, place_ref, *send_refs):
    early = dg(qkv_ref[0], delta[...], 1, 0).T.astype(bf16)
    rows = dg(place_ref[...], early, 0, 0).astype(bf16)
    for s, ref in enumerate(send_refs):
        ref[...] = rows[s * cap : (s + 1) * cap, :]


def join_kernel(group, cap, me_ref, slots_ref, mid_ref, *rest):
    back_refs, input_ref = rest[:group], rest[group]
    slots = slots_ref[...]
    total = jnp.zeros(mid_ref.shape, f32)
    for s in range(group):
        total = total + dg(slot_matrix(slots, s * cap, cap), back_refs[s][...], 0, 0)
    input_ref[...] = (mid_ref[...].astype(f32) + total.astype(bf16).astype(f32)).astype(bf16)


def tree_sum(values):
    while len(values) > 1:
        values = [values[i] + values[i + 1] for i in range(0, len(values), 2)]
    return values[0]


def add_kernel(counts, me_ref, *rest):
    ins, outs = rest[: sum(counts)], rest[sum(counts) :]
    first = at = 0
    for count in counts:
        group = ins[at : at + count]
        rows = group[0].shape[1]
        for j, out in enumerate(outs):
            out[0, first : first + rows, :] = tree_sum([x[j].astype(f32) for x in group]).astype(bf16)
        first, at = first + rows, at + count


def add_parts(me, groups):
    pieces, _, channels = groups[0][0].shape
    rows = sum(g[0].shape[1] for g in groups)
    return call(
        partial(add_kernel, [len(g) for g in groups]),
        [shape((1, rows, channels), bf16)] * pieces,
        [me] + [x for g in groups for x in g],
    )


def finish_kernel(scale, me_ref, *rest):
    refs, (qkv_ref, out_ref, ready, sems) = rest[:-4], rest[-4:]
    me = me_ref[0]
    _, rows, channels = refs[0].shape
    rows = rows // 2

    def each(s, l, act):
        chunk = s ^ me
        part = chunk * rows // channels
        first = pl.multiple_of(chunk * rows % channels, rows)

        @pl.when(part < 3)
        def _():
            column = pl.multiple_of(part * channels, channels)
            to = qkv_ref.at[l, pl.ds(first, rows), pl.ds(column, channels)]
            act(pltpu.make_async_copy(ready.at[s, l], to, sems.at[s, l]))

        @pl.when(part == 3)
        def _():
            to = out_ref.at[l, pl.ds(first, rows), :]
            act(pltpu.make_async_copy(ready.at[s, l], to, sems.at[s, l]))

    work = [(s, l) for s in range(len(refs)) for l in range(2)]
    for s, l in work:
        ready[s, l] = refs[s][0, l * rows : (l + 1) * rows, :].astype(f32) * scale
        each(s, l, lambda copy: copy.start())
    for s, l in work:
        each(s, l, lambda copy: copy.wait())


def swap(x, mask, devices):
    return lax.ppermute(x, AXES, [(d, d ^ mask) for d in range(devices)])


def exchange(blocks, devices):
    return [blocks[0]] + [swap(blocks[s], s, devices) for s in range(1, len(blocks))]


def stage_masks(bits):
    masks = [0]
    for b in bits:
        masks = masks + [m | (1 << b) for m in masks]
    return masks


def on_device(section_input, mid_features, out_grad, to_hilbert, to_zorder, qkv_weight, out_weight):
    devices = lax.axis_size("wide") * lax.axis_size("narrow")
    n, channels = section_input.shape
    group = devices // 8
    share = n // group
    cap = share + 2 * (share // 4)
    rank = (lax.axis_index("wide") * lax.axis_size("narrow") + lax.axis_index("narrow")).astype(i32)
    me = rank.reshape(1)
    blocks = 8
    low = rank % blocks
    place = ((low & 1) << 2 | (low >> 1)).reshape(1)
    bits = devices.bit_length() - 1
    whole_stages = [tuple(range(b, min(b + 2, bits))) for b in range(3, bits, 2)]

    size_rows = shape((n, channels), bf16)
    size_send = shape((cap, channels), bf16)
    some_heads = pltpu.VMEM((KEPT, n, n), bf16)
    powers_s, att_s, inv_s = (HEADS, n, n), (channels, n), (HEADS, n)
    half = shape((blocks // 2, 4 * channels // blocks, channels), bf16)

    moved = [mid_features, out_grad, qkv_weight, out_weight]
    slots, *rest = call(
        partial(route_kernel, group, cap),
        [shape((1, n), i32)]
        + [shape((cap + 16, channels), bf16)] * group
        + [shape(x.shape, bf16) for x in moved],
        [me, to_zorder.reshape(1, n), section_input] + moved,
        [
            pltpu.VMEM((1, n), i32),
            pltpu.VMEM((n, channels), bf16),
            pltpu.VMEM((n, n), bf16),
            pltpu.SemaphoreType.DMA((6,)),
        ],
        us=2,
        in_hbm=6,
    )
    feats = exchange(rest[:group], devices)
    mid_features, out_grad, qkv_w, out_w = rest[group:]
    mid, late_keep, late_send, *grads = call(
        partial(late_kernel, group, cap),
        [size_rows, half, half] + [size_send] * group,
        [place, mid_features, out_grad, qkv_w, out_w, slots],
        [
            pltpu.VMEM((4 * channels, n), bf16),
            pltpu.VMEM((3 * channels, n), bf16),
            some_heads,
            some_heads,
            pltpu.VMEM(att_s, f32),
            pltpu.VMEM(inv_s, f32),
            some_heads,
            some_heads,
        ],
        us=16,
    )
    grads = exchange(grads, devices)
    late_got = swap(late_send, 1, devices)
    place_rows, *layer = call(
        partial(forward_kernel, group, cap),
        [
            shape((n, group * cap), bf16),
            shape((channels, n), bf16),
            shape((3 * channels, n), bf16),
            shape(powers_s, bf16),
            shape(powers_s, bf16),
            shape(att_s, f32),
            shape(inv_s, f32),
        ],
        [me, qkv_w, *feats],
        us=7,
    )
    delta, keep, send = call(
        partial(backward_kernel, group),
        [
            shape((3 * channels, n), bf16),
            half,
            half,
        ],
        [place, out_w, place_rows, *layer, *grads],
        [pltpu.VMEM((channels, n), bf16), some_heads, some_heads],
        us=9,
    )
    got = swap(send, 1, devices)
    backs = call(
        partial(rows_kernel, cap),
        [size_send] * group,
        [me, qkv_w, delta, place_rows],
        us=2,
    )
    pieces = add_parts(me, [[keep, got], [late_keep, late_got]])
    masks = stage_masks((1, 2))
    parts = [pieces[0]] + [swap(pieces[i], masks[i], devices) for i in range(1, 4)]
    (total,) = add_parts(me, [parts])
    backs = exchange(backs, devices)
    for stage in whole_stages:
        parts = [total] + [swap(total, m, devices) for m in stage_masks(stage)[1:]]
        (total,) = add_parts(me, [parts])
    (input_grad,) = call(
        partial(join_kernel, group, cap), [size_rows], [me, slots, mid, *backs]
    )
    total, input_grad = lax.optimization_barrier((total, input_grad))
    parts = [total] + [swap(total, m, devices) for m in masks[1:]]
    parts = parts + [swap(x, 1, devices) for x in parts]
    qkv_grad, out_w_grad = call(
        partial(finish_kernel, float((n * devices) ** -0.5)),
        [shape(qkv_weight.shape, f32), shape(out_weight.shape, f32)],
        [place, *parts],
        [
            pltpu.VMEM((blocks, 2) + half.shape[1:], f32),
            pltpu.SemaphoreType.DMA((blocks, 2)),
        ],
        out=pltpu.HBM,
    )
    return (input_grad, qkv_grad, out_w_grad)


def solution(mesh):
    placed = (
        P(AXES, None),
        P(AXES, None),
        P(AXES, None),
        P(AXES),
        P(AXES),
        P(),
        P(),
    )
    return jax.shard_map(
        on_device,
        mesh=mesh,
        in_specs=placed,
        out_specs=(P(AXES, None), P(), P()),
        check_vma=False,
    )
```

```python
from functools import partial

import jax
import jax.numpy as jnp
from jax import lax
from jax.experimental import pallas as pl
from jax.experimental.pallas import tpu as pltpu
from jax.sharding import PartitionSpec as P

HEADS = 16
LOG2E = 1.4426950408889634
f32, bf16, i32 = jnp.float32, jnp.bfloat16, jnp.int32
AXES = ("wide", "narrow")
VMEM_LIMIT = 26 * 2**20
KEPT = 4


def shape(dims, dtype):
    return jax.ShapeDtypeStruct(tuple(dims), dtype)


def dg(a, b, contract_a, contract_b):
    return lax.dot_general(
        a, b, (((contract_a,), (contract_b,)), ((), ())), preferred_element_type=f32
    )


def call(body, out_shape, args, scratch=(), us=1, in_hbm=0, out=pltpu.VMEM):
    args = list(args)
    for i in range(len(args) - in_hbm, len(args)):
        args[i] = pltpu.with_memory_space_constraint(args[i], pltpu.HBM)
    return pl.pallas_call(
        body,
        out_shape=tuple(out_shape),
        in_specs=[pl.BlockSpec(memory_space=pltpu.SMEM)]
        + [pl.BlockSpec(memory_space=pltpu.VMEM)] * (len(args) - 1 - in_hbm)
        + [pl.BlockSpec(memory_space=pltpu.HBM)] * in_hbm,
        out_specs=tuple([pl.BlockSpec(memory_space=out)] * len(out_shape)),
        scratch_shapes=list(scratch),
        compiler_params=pltpu.CompilerParams(vmem_limit_bytes=VMEM_LIMIT),
        cost_estimate=pl.CostEstimate(flops=us * 10**9, bytes_accessed=2**20, transcendentals=0),
    )(*args)


def slot_matrix(slots, first, count):
    rows = slots.shape[1]
    at = lax.broadcasted_iota(i32, (count, rows), 0) + first
    return jnp.where(at == slots, 1.0, 0.0).astype(bf16)


def place_matrix(spot, n):
    at = lax.broadcasted_iota(i32, (n, spot.shape[1]), 0)
    return jnp.where(at == spot, 1.0, 0.0).astype(bf16)


def placed_rows(place_ref, blocks):
    rows = jnp.concatenate(blocks, axis=0)
    n = place_ref.shape[0]
    halves = [dg(place_ref[i : i + n // 2, :], rows, 1, 0) for i in (0, n // 2)]
    return jnp.concatenate(halves, axis=0).astype(bf16)


def spots_of(recv_ref, cap):
    info = recv_ref[cap : cap + 16, 0:cap].astype(f32)
    spot = info[0:1] + 256.0 * info[1:2] + 1024.0 * (info[2:3] - 1.0)
    return spot.astype(i32)


def route_kernel(group, cap, me_ref, tz_hbm, rows_hbm, h_hbm, g_hbm, qkv_hbm, out_hbm, *rest):
    slots_ref, send_refs = rest[0], rest[1 : 1 + group]
    tz_ref, rows_ref, earlier_ref, sems = rest[5 + group :]
    sources = (tz_hbm, rows_hbm, h_hbm, g_hbm, qkv_hbm, out_hbm)
    targets = (tz_ref, rows_ref) + tuple(rest[1 + group : 5 + group])
    copies = [
        pltpu.make_async_copy(a, b, sems.at[i]) for i, (a, b) in enumerate(zip(sources, targets))
    ]
    for copy in copies:
        copy.start()
    n, channels = rows_ref.shape
    earlier_ref[...] = jnp.where(
        lax.broadcasted_iota(i32, (n, n), 0) < lax.broadcasted_iota(i32, (n, n), 1), 1.0, 0.0
    ).astype(bf16)
    copies[0].wait()
    copies[1].wait()
    here = me_ref[0] % group
    target = tz_ref[...]
    partner = (target // n % group) ^ here
    spot = target % n
    lanes = max(16, group)
    which = lax.broadcasted_iota(i32, (lanes, n), 0)
    mine = jnp.where(which == partner, 1.0, 0.0)
    before = dg(mine.astype(bf16), earlier_ref[...], 1, 0)
    rank = jnp.sum(mine * before, axis=0, keepdims=True).astype(i32)
    slots = partner * cap + rank
    slots_ref[...] = slots
    row_at = lax.broadcasted_iota(i32, (16, n), 0)
    info = jnp.where(
        row_at == 0, spot % 256, jnp.where(row_at == 1, spot // 256, (row_at == 2).astype(i32))
    ).astype(f32).astype(bf16)
    rows = rows_ref[...]
    for s in range(group):
        chosen = slot_matrix(slots, s * cap, cap)
        send_refs[s][0:cap, :] = dg(chosen, rows, 1, 0).astype(bf16)
        where = dg(info, chosen, 1, 1)
        if cap < channels:
            where = jnp.concatenate([where, jnp.zeros((16, channels - cap), f32)], axis=1)
        send_refs[s][cap : cap + 16, :] = where.astype(bf16)
    for copy in copies[2:]:
        copy.wait()


def three_terms(x):
    parts = []
    for _ in range(3):
        parts.append(x.astype(bf16))
        x = x - parts[-1].astype(f32)
    return jnp.concatenate(parts, axis=0)


class Heads:

    def __init__(self, channels, proj, out_delta, delta, powers, turned, att, inv, grads, turned_grads):
        self.channels, self.size = channels, channels // HEADS
        self.proj, self.out_delta, self.delta = proj, out_delta, delta
        self.powers, self.turned, self.att, self.inv = powers, turned, att, inv
        self.grads, self.turned_grads = grads, turned_grads
        self.held = {}

    def rows(self, ref, part, head):
        first = part * self.channels + head * self.size
        return ref[first : first + self.size, :]

    def scores(self, head):
        k = self.rows(self.proj, 1, head)
        q = self.rows(self.proj, 0, head).astype(f32) * (self.size**-0.5 * LOG2E)
        self.held["s", head] = dg(jnp.concatenate([k] * 3, axis=0), three_terms(q), 0, 0)

    def softmax(self, head):
        scores = self.held.pop(("s", head))
        powers = jnp.exp2(scores - jnp.max(scores, axis=0, keepdims=True))
        self.powers[head % self.powers.shape[0]] = powers.astype(bf16)
        self.inv[head : head + 1, :] = 1.0 / jnp.sum(powers, axis=0, keepdims=True)

    def attend(self, head):
        slot = head % self.powers.shape[0]
        powers = self.powers[slot]
        first = head * self.size
        self.att[first : first + self.size, :] = (
            dg(self.rows(self.proj, 2, head), powers, 1, 0) * self.inv[head : head + 1, :]
        )
        self.turned[slot] = powers.T

    def prob_grad(self, head):
        o = self.rows(self.out_delta, 0, head).astype(f32)
        inverse = self.inv[head : head + 1, :]
        centre = jnp.sum(self.rows(self.att, 0, head) * o, axis=0, keepdims=True) * inverse
        v = self.rows(self.proj, 2, head)
        o = three_terms(o * inverse)
        self.held["p", head] = dg(jnp.concatenate([v] * 3, axis=0), o, 0, 0) - centre
        self.held["o", head] = o[0 : 2 * self.size]

    def score_grad(self, head):
        slot = head % self.grads.shape[0]
        powers = self.powers[head % self.powers.shape[0]].astype(f32)
        grad = (powers * self.held.pop(("p", head))).astype(bf16)
        self.grads[slot] = grad
        self.turned_grads[slot] = grad.T

    def products(self, head):
        slot = head % self.grads.shape[0]
        scale = self.size**-0.5
        value = dg(self.held.pop(("o", head)), self.turned[head % self.turned.shape[0]], 1, 0)
        query = dg(self.rows(self.proj, 1, head), self.grads[slot], 1, 0) * scale
        key = dg(self.rows(self.proj, 0, head), self.turned_grads[slot], 1, 0) * scale
        value = value[0 : self.size] + value[self.size :]
        for part, grad in enumerate((query, key, value)):
            first = part * self.channels + head * self.size
            self.delta[first : first + self.size, :] = grad.astype(bf16)


def pipeline(*stages):
    for step in range(HEADS + max(lag for _, lag in stages)):
        for work, lag in stages:
            if 0 <= step - lag < HEADS:
                work(step - lag)


def store_blocks(me, qkv_grad, out_grad, keep_ref, send_ref):
    half, rows, channels = keep_ref.shape

    def store(first_ref, second_ref):
        for c in range(2 * half):
            ref = first_ref if c < half else second_ref
            part, first = c * rows // channels, c * rows % channels
            if part < 3:
                piece = qkv_grad[first : first + rows, part * channels : (part + 1) * channels]
            else:
                piece = out_grad[first : first + rows, :]
            ref[(c ^ me) % half] = piece

    @pl.when(me < half)
    def _():
        store(keep_ref, send_ref)

    @pl.when(me >= half)
    def _():
        store(send_ref, keep_ref)


def late_kernel(group, cap, me_ref, h_ref, g_ref, qkv_ref, out_ref, slots_ref, *rest):
    mid_ref, keep_ref, send_ref = rest[0:3]
    send_refs = rest[3 : 3 + group]
    proj, delta, powers, turned, att_ref, inv_ref, grads, turned_grads = rest[3 + group :]
    h, g = h_ref[...], g_ref[...]
    n, channels = h.shape
    qkv_w = qkv_ref[1]
    proj[0 : 3 * channels, :] = dg(qkv_w, h, 0, 1).astype(bf16)
    proj[3 * channels : 4 * channels, :] = dg(out_ref[1], g, 1, 1).astype(bf16)
    out_delta = proj.at[3 * channels : 4 * channels, :]
    heads = Heads(
        channels, proj, out_delta, delta, powers, turned, att_ref, inv_ref, grads, turned_grads
    )
    pipeline(
        (heads.scores, 0),
        (heads.score_grad, 3),
        (heads.softmax, 1),
        (heads.products, 4),
        (heads.attend, 2),
        (heads.prob_grad, 2),
    )
    qkv_delta = delta[...]
    row_grad = dg(qkv_w, qkv_delta, 1, 0).T
    mid = (g.astype(f32) + row_grad).astype(bf16)
    mid_ref[...] = mid
    slots = slots_ref[...]
    for s in range(group):
        send_refs[s][...] = dg(slot_matrix(slots, s * cap, cap), mid, 1, 0).astype(bf16)
    qkv_grad = dg(h.T, qkv_delta, 1, 1).astype(bf16)
    out_grad = dg(att_ref[...].astype(bf16), g, 1, 0).astype(bf16)
    store_blocks(me_ref[0], qkv_grad, out_grad, keep_ref, send_ref)


def forward_kernel(group, cap, me_ref, qkv_ref, *rest):
    feats_refs = rest[0:group]
    place_ref, turned_h_ref, proj, powers, turned, att_ref, inv_ref = rest[group:]
    channels, n = turned_h_ref.shape
    spots = jnp.concatenate([spots_of(ref, cap) for ref in feats_refs], axis=1)
    place_ref[...] = place_matrix(spots, n)
    h = placed_rows(place_ref, [ref[0:cap, :] for ref in feats_refs])
    turned_h_ref[...] = h.T
    for part in range(3):
        rows = slice(part * channels, (part + 1) * channels)
        proj[rows, :] = dg(qkv_ref[0, :, rows], turned_h_ref[...], 0, 0).astype(bf16)
    heads = Heads(channels, proj, None, None, powers, turned, att_ref, inv_ref, None, None)
    pipeline((heads.softmax, 1), (heads.scores, 0), (heads.attend, 2))


def backward_kernel(group, me_ref, out_ref, place_ref, turned_h_ref, proj, *rest):
    powers, turned, att_ref, inv_ref = rest[0:4]
    grads_refs = rest[4 : 4 + group]
    delta, keep_ref, send_ref, out_delta, grads, turned_grads = rest[4 + group :]
    channels, n = turned_h_ref.shape
    g = placed_rows(place_ref, [ref[...] for ref in grads_refs])
    out_delta[...] = dg(out_ref[0], g, 1, 1).astype(bf16)
    heads = Heads(
        channels, proj, out_delta, delta, powers, turned, att_ref, inv_ref, grads, turned_grads
    )
    pipeline((heads.score_grad, 1), (heads.prob_grad, 0), (heads.products, 2))
    qkv_grad = dg(turned_h_ref[...], delta[...], 1, 1).astype(bf16)
    out_grad = dg(att_ref[...].astype(bf16), g, 1, 0).astype(bf16)
    store_blocks(me_ref[0], qkv_grad, out_grad, keep_ref, send_ref)


def rows_kernel(cap, me_ref, qkv_ref, delta, place_ref, *send_refs):
    early = dg(qkv_ref[0], delta[...], 1, 0).T.astype(bf16)
    rows = dg(place_ref[...], early, 0, 0).astype(bf16)
    for s, ref in enumerate(send_refs):
        ref[...] = rows[s * cap : (s + 1) * cap, :]


def join_kernel(group, cap, me_ref, slots_ref, mid_ref, *rest):
    back_refs, input_ref = rest[:group], rest[group]
    slots = slots_ref[...]
    total = jnp.zeros(mid_ref.shape, f32)
    for s in range(group):
        total = total + dg(slot_matrix(slots, s * cap, cap), back_refs[s][...], 0, 0)
    input_ref[...] = (mid_ref[...].astype(f32) + total.astype(bf16).astype(f32)).astype(bf16)


def tree_sum(values):
    while len(values) > 1:
        values = [values[i] + values[i + 1] for i in range(0, len(values), 2)]
    return values[0]


def add_kernel(counts, me_ref, *rest):
    ins, outs = rest[: sum(counts)], rest[sum(counts) :]
    first = at = 0
    for count in counts:
        group = ins[at : at + count]
        rows = group[0].shape[1]
        for j, out in enumerate(outs):
            out[0, first : first + rows, :] = tree_sum([x[j].astype(f32) for x in group]).astype(bf16)
        first, at = first + rows, at + count


def add_parts(me, groups):
    pieces, _, channels = groups[0][0].shape
    rows = sum(g[0].shape[1] for g in groups)
    return call(
        partial(add_kernel, [len(g) for g in groups]),
        [shape((1, rows, channels), bf16)] * pieces,
        [me] + [x for g in groups for x in g],
    )


def finish_kernel(scale, me_ref, *rest):
    refs, (qkv_ref, out_ref, ready, sems) = rest[:-4], rest[-4:]
    me = me_ref[0]
    _, rows, channels = refs[0].shape
    rows = rows // 2

    def each(s, l, act):
        chunk = s ^ me
        part = chunk * rows // channels
        first = pl.multiple_of(chunk * rows % channels, rows)

        @pl.when(part < 3)
        def _():
            column = pl.multiple_of(part * channels, channels)
            to = qkv_ref.at[l, pl.ds(first, rows), pl.ds(column, channels)]
            act(pltpu.make_async_copy(ready.at[s, l], to, sems.at[s, l]))

        @pl.when(part == 3)
        def _():
            to = out_ref.at[l, pl.ds(first, rows), :]
            act(pltpu.make_async_copy(ready.at[s, l], to, sems.at[s, l]))

    work = [(s, l) for s in range(len(refs)) for l in range(2)]
    for s, l in work:
        ready[s, l] = refs[s][0, l * rows : (l + 1) * rows, :].astype(f32) * scale
        each(s, l, lambda copy: copy.start())
    for s, l in work:
        each(s, l, lambda copy: copy.wait())


def swap(x, mask, devices):
    return lax.ppermute(x, AXES, [(d, d ^ mask) for d in range(devices)])


def exchange(blocks, devices):
    return [blocks[0]] + [swap(blocks[s], s, devices) for s in range(1, len(blocks))]


def stage_masks(bits):
    masks = [0]
    for b in bits:
        masks = masks + [m | (1 << b) for m in masks]
    return masks


def on_device(section_input, mid_features, out_grad, to_hilbert, to_zorder, qkv_weight, out_weight):
    devices = lax.axis_size("wide") * lax.axis_size("narrow")
    n, channels = section_input.shape
    group = devices // 8
    share = n // group
    cap = share + 2 * (share // 4)
    rank = (lax.axis_index("wide") * lax.axis_size("narrow") + lax.axis_index("narrow")).astype(i32)
    me = rank.reshape(1)
    blocks = 8
    low = rank % blocks
    place = ((low & 1) << 2 | (low >> 1)).reshape(1)
    bits = devices.bit_length() - 1
    whole_stages = [(b,) for b in reversed(range(3, bits))]

    size_rows = shape((n, channels), bf16)
    size_send = shape((cap, channels), bf16)
    some_heads = pltpu.VMEM((KEPT, n, n), bf16)
    powers_s, att_s, inv_s = (HEADS, n, n), (channels, n), (HEADS, n)
    half = shape((blocks // 2, 4 * channels // blocks, channels), bf16)

    moved = [mid_features, out_grad, qkv_weight, out_weight]
    slots, *rest = call(
        partial(route_kernel, group, cap),
        [shape((1, n), i32)]
        + [shape((cap + 16, channels), bf16)] * group
        + [shape(x.shape, bf16) for x in moved],
        [me, to_zorder.reshape(1, n), section_input] + moved,
        [
            pltpu.VMEM((1, n), i32),
            pltpu.VMEM((n, channels), bf16),
            pltpu.VMEM((n, n), bf16),
            pltpu.SemaphoreType.DMA((6,)),
        ],
        us=2,
        in_hbm=6,
    )
    feats = exchange(rest[:group], devices)
    mid_features, out_grad, qkv_w, out_w = rest[group:]
    mid, late_keep, late_send, *grads = call(
        partial(late_kernel, group, cap),
        [size_rows, half, half] + [size_send] * group,
        [place, mid_features, out_grad, qkv_w, out_w, slots],
        [
            pltpu.VMEM((4 * channels, n), bf16),
            pltpu.VMEM((3 * channels, n), bf16),
            some_heads,
            some_heads,
            pltpu.VMEM(att_s, f32),
            pltpu.VMEM(inv_s, f32),
            some_heads,
            some_heads,
        ],
        us=16,
    )
    grads = exchange(grads, devices)
    late_got = swap(late_send, 1, devices)
    place_rows, *layer = call(
        partial(forward_kernel, group, cap),
        [
            shape((n, group * cap), bf16),
            shape((channels, n), bf16),
            shape((3 * channels, n), bf16),
            shape(powers_s, bf16),
            shape(powers_s, bf16),
            shape(att_s, f32),
            shape(inv_s, f32),
        ],
        [me, qkv_w, *feats],
        us=7,
    )
    delta, keep, send = call(
        partial(backward_kernel, group),
        [
            shape((3 * channels, n), bf16),
            half,
            half,
        ],
        [place, out_w, place_rows, *layer, *grads],
        [pltpu.VMEM((channels, n), bf16), some_heads, some_heads],
        us=9,
    )
    got = swap(send, 1, devices)
    backs = call(
        partial(rows_kernel, cap),
        [size_send] * group,
        [me, qkv_w, delta, place_rows],
        us=2,
    )
    pieces = add_parts(me, [[keep, got], [late_keep, late_got]])
    masks = stage_masks((1, 2))
    parts = [pieces[0]] + [swap(pieces[i], masks[i], devices) for i in range(1, 4)]
    (total,) = add_parts(me, [parts])
    backs = exchange(backs, devices)
    for stage in whole_stages:
        parts = [total] + [swap(total, m, devices) for m in stage_masks(stage)[1:]]
        (total,) = add_parts(me, [parts])
    (input_grad,) = call(
        partial(join_kernel, group, cap), [size_rows], [me, slots, mid, *backs]
    )
    total, input_grad = lax.optimization_barrier((total, input_grad))
    parts = [total] + [swap(total, m, devices) for m in masks[1:]]
    parts = parts + [swap(x, 1, devices) for x in parts]
    qkv_grad, out_w_grad = call(
        partial(finish_kernel, float((n * devices) ** -0.5)),
        [shape(qkv_weight.shape, f32), shape(out_weight.shape, f32)],
        [place, *parts],
        [
            pltpu.VMEM((blocks, 2) + half.shape[1:], f32),
            pltpu.SemaphoreType.DMA((blocks, 2)),
        ],
        out=pltpu.HBM,
    )
    return (input_grad, qkv_grad, out_w_grad)


def solution(mesh):
    placed = (
        P(AXES, None),
        P(AXES, None),
        P(AXES, None),
        P(AXES),
        P(AXES),
        P(),
        P(),
    )
    return jax.shard_map(
        on_device,
        mesh=mesh,
        in_specs=placed,
        out_specs=(P(AXES, None), P(), P()),
        check_vma=False,
    )
```

```python
from functools import partial

import jax
import jax.numpy as jnp
from jax import lax
from jax.experimental import pallas as pl
from jax.experimental.pallas import tpu as pltpu
from jax.sharding import PartitionSpec as P

HEADS = 16
LOG2E = 1.4426950408889634
f32, bf16, i32 = jnp.float32, jnp.bfloat16, jnp.int32
AXES = ("wide", "narrow")
VMEM_LIMIT = 26 * 2**20
KEPT = 4


def shape(dims, dtype):
    return jax.ShapeDtypeStruct(tuple(dims), dtype)


def dg(a, b, contract_a, contract_b):
    return lax.dot_general(
        a, b, (((contract_a,), (contract_b,)), ((), ())), preferred_element_type=f32
    )


def call(body, out_shape, args, scratch=(), us=1, in_hbm=0, out=pltpu.VMEM):
    args = list(args)
    for i in range(len(args) - in_hbm, len(args)):
        args[i] = pltpu.with_memory_space_constraint(args[i], pltpu.HBM)
    return pl.pallas_call(
        body,
        out_shape=tuple(out_shape),
        in_specs=[pl.BlockSpec(memory_space=pltpu.SMEM)]
        + [pl.BlockSpec(memory_space=pltpu.VMEM)] * (len(args) - 1 - in_hbm)
        + [pl.BlockSpec(memory_space=pltpu.HBM)] * in_hbm,
        out_specs=tuple([pl.BlockSpec(memory_space=out)] * len(out_shape)),
        scratch_shapes=list(scratch),
        compiler_params=pltpu.CompilerParams(vmem_limit_bytes=VMEM_LIMIT),
        cost_estimate=pl.CostEstimate(flops=us * 10**9, bytes_accessed=2**20, transcendentals=0),
    )(*args)


def slot_matrix(slots, first, count):
    rows = slots.shape[1]
    at = lax.broadcasted_iota(i32, (count, rows), 0) + first
    return jnp.where(at == slots, 1.0, 0.0).astype(bf16)


def place_matrix(spot, n):
    at = lax.broadcasted_iota(i32, (n, spot.shape[1]), 0)
    return jnp.where(at == spot, 1.0, 0.0).astype(bf16)


def placed_rows(place_ref, blocks):
    rows = jnp.concatenate(blocks, axis=0)
    n = place_ref.shape[0]
    halves = [dg(place_ref[i : i + n // 2, :], rows, 1, 0) for i in (0, n // 2)]
    return jnp.concatenate(halves, axis=0).astype(bf16)


def spots_of(recv_ref, cap):
    info = recv_ref[cap : cap + 16, 0:cap].astype(f32)
    spot = info[0:1] + 256.0 * info[1:2] + 1024.0 * (info[2:3] - 1.0)
    return spot.astype(i32)


def route_kernel(group, cap, me_ref, tz_hbm, rows_hbm, h_hbm, g_hbm, qkv_hbm, out_hbm, *rest):
    slots_ref, send_refs = rest[0], rest[1 : 1 + group]
    tz_ref, rows_ref, earlier_ref, sems = rest[5 + group :]
    sources = (tz_hbm, rows_hbm, h_hbm, g_hbm, qkv_hbm, out_hbm)
    targets = (tz_ref, rows_ref) + tuple(rest[1 + group : 5 + group])
    copies = [
        pltpu.make_async_copy(a, b, sems.at[i]) for i, (a, b) in enumerate(zip(sources, targets))
    ]
    for copy in copies:
        copy.start()
    n, channels = rows_ref.shape
    earlier_ref[...] = jnp.where(
        lax.broadcasted_iota(i32, (n, n), 0) < lax.broadcasted_iota(i32, (n, n), 1), 1.0, 0.0
    ).astype(bf16)
    copies[0].wait()
    copies[1].wait()
    here = me_ref[0] % group
    target = tz_ref[...]
    partner = (target // n % group) ^ here
    spot = target % n
    lanes = max(16, group)
    which = lax.broadcasted_iota(i32, (lanes, n), 0)
    mine = jnp.where(which == partner, 1.0, 0.0)
    before = dg(mine.astype(bf16), earlier_ref[...], 1, 0)
    rank = jnp.sum(mine * before, axis=0, keepdims=True).astype(i32)
    slots = partner * cap + rank
    slots_ref[...] = slots
    row_at = lax.broadcasted_iota(i32, (16, n), 0)
    info = jnp.where(
        row_at == 0, spot % 256, jnp.where(row_at == 1, spot // 256, (row_at == 2).astype(i32))
    ).astype(f32).astype(bf16)
    rows = rows_ref[...]
    for s in range(group):
        chosen = slot_matrix(slots, s * cap, cap)
        send_refs[s][0:cap, :] = dg(chosen, rows, 1, 0).astype(bf16)
        where = dg(info, chosen, 1, 1)
        if cap < channels:
            where = jnp.concatenate([where, jnp.zeros((16, channels - cap), f32)], axis=1)
        send_refs[s][cap : cap + 16, :] = where.astype(bf16)
    for copy in copies[2:]:
        copy.wait()


def three_terms(x):
    parts = []
    for _ in range(3):
        parts.append(x.astype(bf16))
        x = x - parts[-1].astype(f32)
    return jnp.concatenate(parts, axis=0)


class Heads:

    def __init__(self, channels, proj, out_delta, delta, powers, turned, att, inv, grads, turned_grads):
        self.channels, self.size = channels, channels // HEADS
        self.proj, self.out_delta, self.delta = proj, out_delta, delta
        self.powers, self.turned, self.att, self.inv = powers, turned, att, inv
        self.grads, self.turned_grads = grads, turned_grads
        self.held = {}

    def rows(self, ref, part, head):
        first = part * self.channels + head * self.size
        return ref[first : first + self.size, :]

    def scores(self, head):
        k = self.rows(self.proj, 1, head)
        q = self.rows(self.proj, 0, head).astype(f32) * (self.size**-0.5 * LOG2E)
        self.held["s", head] = dg(jnp.concatenate([k] * 3, axis=0), three_terms(q), 0, 0)

    def softmax(self, head):
        scores = self.held.pop(("s", head))
        powers = jnp.exp2(scores - jnp.max(scores, axis=0, keepdims=True))
        self.powers[head % self.powers.shape[0]] = powers.astype(bf16)
        self.inv[head : head + 1, :] = 1.0 / jnp.sum(powers, axis=0, keepdims=True)

    def attend(self, head):
        slot = head % self.powers.shape[0]
        powers = self.powers[slot]
        first = head * self.size
        self.att[first : first + self.size, :] = (
            dg(self.rows(self.proj, 2, head), powers, 1, 0) * self.inv[head : head + 1, :]
        )
        self.turned[slot] = powers.T

    def prob_grad(self, head):
        o = self.rows(self.out_delta, 0, head).astype(f32)
        inverse = self.inv[head : head + 1, :]
        centre = jnp.sum(self.rows(self.att, 0, head) * o, axis=0, keepdims=True) * inverse
        v = self.rows(self.proj, 2, head)
        o = three_terms(o * inverse)
        self.held["p", head] = dg(jnp.concatenate([v] * 3, axis=0), o, 0, 0) - centre
        self.held["o", head] = o[0 : 2 * self.size]

    def score_grad(self, head):
        slot = head % self.grads.shape[0]
        powers = self.powers[head % self.powers.shape[0]].astype(f32)
        grad = (powers * self.held.pop(("p", head))).astype(bf16)
        self.grads[slot] = grad
        self.turned_grads[slot] = grad.T

    def products(self, head):
        slot = head % self.grads.shape[0]
        scale = self.size**-0.5
        value = dg(self.held.pop(("o", head)), self.turned[head % self.turned.shape[0]], 1, 0)
        query = dg(self.rows(self.proj, 1, head), self.grads[slot], 1, 0) * scale
        key = dg(self.rows(self.proj, 0, head), self.turned_grads[slot], 1, 0) * scale
        value = value[0 : self.size] + value[self.size :]
        for part, grad in enumerate((query, key, value)):
            first = part * self.channels + head * self.size
            self.delta[first : first + self.size, :] = grad.astype(bf16)


def pipeline(*stages):
    for step in range(HEADS + max(lag for _, lag in stages)):
        for work, lag in stages:
            if 0 <= step - lag < HEADS:
                work(step - lag)


def store_blocks(me, qkv_grad, out_grad, keep_ref, send_ref):
    half, rows, channels = keep_ref.shape

    def store(first_ref, second_ref):
        for c in range(2 * half):
            ref = first_ref if c < half else second_ref
            part, first = c * rows // channels, c * rows % channels
            if part < 3:
                piece = qkv_grad[first : first + rows, part * channels : (part + 1) * channels]
            else:
                piece = out_grad[first : first + rows, :]
            ref[(c ^ me) % half] = piece

    @pl.when(me < half)
    def _():
        store(keep_ref, send_ref)

    @pl.when(me >= half)
    def _():
        store(send_ref, keep_ref)


def late_kernel(group, cap, me_ref, h_ref, g_ref, qkv_ref, out_ref, slots_ref, *rest):
    mid_ref, keep_ref, send_ref = rest[0:3]
    send_refs = rest[3 : 3 + group]
    proj, delta, powers, turned, att_ref, inv_ref, grads, turned_grads = rest[3 + group :]
    h, g = h_ref[...], g_ref[...]
    n, channels = h.shape
    qkv_w = qkv_ref[1]
    proj[0 : 3 * channels, :] = dg(qkv_w, h, 0, 1).astype(bf16)
    proj[3 * channels : 4 * channels, :] = dg(out_ref[1], g, 1, 1).astype(bf16)
    out_delta = proj.at[3 * channels : 4 * channels, :]
    heads = Heads(
        channels, proj, out_delta, delta, powers, turned, att_ref, inv_ref, grads, turned_grads
    )
    pipeline(
        (heads.scores, 0),
        (heads.score_grad, 3),
        (heads.softmax, 1),
        (heads.products, 4),
        (heads.attend, 2),
        (heads.prob_grad, 2),
    )
    qkv_delta = delta[...]
    row_grad = dg(qkv_w, qkv_delta, 1, 0).T
    mid = (g.astype(f32) + row_grad).astype(bf16)
    mid_ref[...] = mid
    slots = slots_ref[...]
    for s in range(group):
        send_refs[s][...] = dg(slot_matrix(slots, s * cap, cap), mid, 1, 0).astype(bf16)
    qkv_grad = dg(h.T, qkv_delta, 1, 1).astype(bf16)
    out_grad = dg(att_ref[...].astype(bf16), g, 1, 0).astype(bf16)
    store_blocks(me_ref[0], qkv_grad, out_grad, keep_ref, send_ref)


def forward_kernel(group, cap, me_ref, qkv_ref, *rest):
    feats_refs = rest[0:group]
    place_ref, turned_h_ref, proj, powers, turned, att_ref, inv_ref = rest[group:]
    channels, n = turned_h_ref.shape
    spots = jnp.concatenate([spots_of(ref, cap) for ref in feats_refs], axis=1)
    place_ref[...] = place_matrix(spots, n)
    h = placed_rows(place_ref, [ref[0:cap, :] for ref in feats_refs])
    turned_h_ref[...] = h.T
    for part in range(3):
        rows = slice(part * channels, (part + 1) * channels)
        proj[rows, :] = dg(qkv_ref[0, :, rows], turned_h_ref[...], 0, 0).astype(bf16)
    heads = Heads(channels, proj, None, None, powers, turned, att_ref, inv_ref, None, None)
    pipeline((heads.softmax, 1), (heads.scores, 0), (heads.attend, 2))


def backward_kernel(group, me_ref, out_ref, place_ref, turned_h_ref, proj, *rest):
    powers, turned, att_ref, inv_ref = rest[0:4]
    grads_refs = rest[4 : 4 + group]
    delta, keep_ref, send_ref, out_delta, grads, turned_grads = rest[4 + group :]
    channels, n = turned_h_ref.shape
    g = placed_rows(place_ref, [ref[...] for ref in grads_refs])
    out_delta[...] = dg(out_ref[0], g, 1, 1).astype(bf16)
    heads = Heads(
        channels, proj, out_delta, delta, powers, turned, att_ref, inv_ref, grads, turned_grads
    )
    pipeline((heads.score_grad, 1), (heads.prob_grad, 0), (heads.products, 2))
    qkv_grad = dg(turned_h_ref[...], delta[...], 1, 1).astype(bf16)
    out_grad = dg(att_ref[...].astype(bf16), g, 1, 0).astype(bf16)
    store_blocks(me_ref[0], qkv_grad, out_grad, keep_ref, send_ref)


def rows_kernel(cap, me_ref, qkv_ref, delta, place_ref, *send_refs):
    early = dg(qkv_ref[0], delta[...], 1, 0).T.astype(bf16)
    rows = dg(place_ref[...], early, 0, 0).astype(bf16)
    for s, ref in enumerate(send_refs):
        ref[...] = rows[s * cap : (s + 1) * cap, :]


def join_kernel(group, cap, me_ref, slots_ref, mid_ref, *rest):
    back_refs, input_ref = rest[:group], rest[group]
    slots = slots_ref[...]
    total = jnp.zeros(mid_ref.shape, f32)
    for s in range(group):
        total = total + dg(slot_matrix(slots, s * cap, cap), back_refs[s][...], 0, 0)
    input_ref[...] = (mid_ref[...].astype(f32) + total.astype(bf16).astype(f32)).astype(bf16)


def tree_sum(values):
    while len(values) > 1:
        values = [values[i] + values[i + 1] for i in range(0, len(values), 2)]
    return values[0]


def add_kernel(counts, me_ref, *rest):
    ins, outs = rest[: sum(counts)], rest[sum(counts) :]
    first = at = 0
    for count in counts:
        group = ins[at : at + count]
        rows = group[0].shape[1]
        for j, out in enumerate(outs):
            out[0, first : first + rows, :] = tree_sum([x[j].astype(f32) for x in group]).astype(bf16)
        first, at = first + rows, at + count


def add_parts(me, groups):
    pieces, _, channels = groups[0][0].shape
    rows = sum(g[0].shape[1] for g in groups)
    return call(
        partial(add_kernel, [len(g) for g in groups]),
        [shape((1, rows, channels), bf16)] * pieces,
        [me] + [x for g in groups for x in g],
    )


def finish_kernel(scale, me_ref, *rest):
    refs, (qkv_ref, out_ref, ready, sems) = rest[:-4], rest[-4:]
    me = me_ref[0]
    _, rows, channels = refs[0].shape
    rows = rows // 2

    def each(s, l, act):
        chunk = s ^ me
        part = chunk * rows // channels
        first = pl.multiple_of(chunk * rows % channels, rows)

        @pl.when(part < 3)
        def _():
            column = pl.multiple_of(part * channels, channels)
            to = qkv_ref.at[l, pl.ds(first, rows), pl.ds(column, channels)]
            act(pltpu.make_async_copy(ready.at[s, l], to, sems.at[s, l]))

        @pl.when(part == 3)
        def _():
            to = out_ref.at[l, pl.ds(first, rows), :]
            act(pltpu.make_async_copy(ready.at[s, l], to, sems.at[s, l]))

    work = [(s, l) for s in range(len(refs)) for l in range(2)]
    for s, l in work:
        ready[s, l] = refs[s][0, l * rows : (l + 1) * rows, :].astype(f32) * scale
        each(s, l, lambda copy: copy.start())
    for s, l in work:
        each(s, l, lambda copy: copy.wait())


def swap(x, mask, devices):
    return lax.ppermute(x, AXES, [(d, d ^ mask) for d in range(devices)])


def exchange(blocks, devices):
    return [blocks[0]] + [swap(blocks[s], s, devices) for s in range(1, len(blocks))]


def stage_masks(bits):
    masks = [0]
    for b in bits:
        masks = masks + [m | (1 << b) for m in masks]
    return masks


def on_device(section_input, mid_features, out_grad, to_hilbert, to_zorder, qkv_weight, out_weight):
    devices = lax.axis_size("wide") * lax.axis_size("narrow")
    n, channels = section_input.shape
    group = devices // 8
    share = n // group
    cap = share + 2 * (share // 4)
    rank = (lax.axis_index("wide") * lax.axis_size("narrow") + lax.axis_index("narrow")).astype(i32)
    me = rank.reshape(1)
    blocks = 8
    low = rank % blocks
    place = ((low & 1) << 2 | (low >> 1)).reshape(1)
    bits = devices.bit_length() - 1
    whole_stages = [(b,) for b in reversed(range(3, bits))]

    size_rows = shape((n, channels), bf16)
    size_send = shape((cap, channels), bf16)
    some_heads = pltpu.VMEM((KEPT, n, n), bf16)
    powers_s, att_s, inv_s = (HEADS, n, n), (channels, n), (HEADS, n)
    half = shape((blocks // 2, 4 * channels // blocks, channels), bf16)

    moved = [mid_features, out_grad, qkv_weight, out_weight]
    slots, *rest = call(
        partial(route_kernel, group, cap),
        [shape((1, n), i32)]
        + [shape((cap + 16, channels), bf16)] * group
        + [shape(x.shape, bf16) for x in moved],
        [me, to_zorder.reshape(1, n), section_input] + moved,
        [
            pltpu.VMEM((1, n), i32),
            pltpu.VMEM((n, channels), bf16),
            pltpu.VMEM((n, n), bf16),
            pltpu.SemaphoreType.DMA((6,)),
        ],
        us=2,
        in_hbm=6,
    )
    feats = exchange(rest[:group], devices)
    mid_features, out_grad, qkv_w, out_w = rest[group:]
    mid, late_keep, late_send, *grads = call(
        partial(late_kernel, group, cap),
        [size_rows, half, half] + [size_send] * group,
        [place, mid_features, out_grad, qkv_w, out_w, slots],
        [
            pltpu.VMEM((4 * channels, n), bf16),
            pltpu.VMEM((3 * channels, n), bf16),
            some_heads,
            some_heads,
            pltpu.VMEM(att_s, f32),
            pltpu.VMEM(inv_s, f32),
            some_heads,
            some_heads,
        ],
        us=16,
    )
    grads = exchange(grads, devices)
    late_got = swap(late_send, 1, devices)
    place_rows, *layer = call(
        partial(forward_kernel, group, cap),
        [
            shape((n, group * cap), bf16),
            shape((channels, n), bf16),
            shape((3 * channels, n), bf16),
            shape(powers_s, bf16),
            shape(powers_s, bf16),
            shape(att_s, f32),
            shape(inv_s, f32),
        ],
        [me, qkv_w, *feats],
        us=7,
    )
    delta, keep, send = call(
        partial(backward_kernel, group),
        [
            shape((3 * channels, n), bf16),
            half,
            half,
        ],
        [place, out_w, place_rows, *layer, *grads],
        [pltpu.VMEM((channels, n), bf16), some_heads, some_heads],
        us=9,
    )
    got = swap(send, 1, devices)
    backs = call(
        partial(rows_kernel, cap),
        [size_send] * group,
        [me, qkv_w, delta, place_rows],
        us=2,
    )
    pieces = add_parts(me, [[keep, got], [late_keep, late_got]])
    masks = stage_masks((1, 2))
    parts = [pieces[0]] + [swap(pieces[i], masks[i], devices) for i in range(1, 4)]
    (total,) = add_parts(me, [parts])
    backs = exchange(backs, devices)
    for stage in whole_stages:
        parts = [total] + [swap(total, m, devices) for m in stage_masks(stage)[1:]]
        (total,) = add_parts(me, [parts])
    total, *backs = lax.optimization_barrier((total, *backs))
    (input_grad,) = call(
        partial(join_kernel, group, cap), [size_rows], [me, slots, mid, *backs]
    )
    parts = [total] + [swap(total, m, devices) for m in masks[1:]]
    parts = parts + [swap(x, 1, devices) for x in parts]
    qkv_grad, out_w_grad = call(
        partial(finish_kernel, float((n * devices) ** -0.5)),
        [shape(qkv_weight.shape, f32), shape(out_weight.shape, f32)],
        [place, *parts],
        [
            pltpu.VMEM((blocks, 2) + half.shape[1:], f32),
            pltpu.SemaphoreType.DMA((blocks, 2)),
        ],
        out=pltpu.HBM,
    )
    return (input_grad, qkv_grad, out_w_grad)


def solution(mesh):
    placed = (
        P(AXES, None),
        P(AXES, None),
        P(AXES, None),
        P(AXES),
        P(AXES),
        P(),
        P(),
    )
    return jax.shard_map(
        on_device,
        mesh=mesh,
        in_specs=placed,
        out_specs=(P(AXES, None), P(), P()),
        check_vma=False,
    )
```
